32 devices in a mesh: dp: 8 (over y, x, core), expert: 4 (over z).
Axes of the slice: x: 2, y: 2, z: 4, core: 2. Of those that a mesh axis runs over, the one named last changes fastest.
Arguments:
- tokens: bfloat16 [4096, 4096], P(('dp', 'expert')), may hold values from -6 to 6
- out_grad: bfloat16 [4096, 4096], P(('dp', 'expert')), may hold values from -6 to 6
- routes: int32 [4096, 2], P(('dp', 'expert')), may hold values from 0 to 3, all different within a row; in each aligned block of 128 rows (0 to 127, 128 to 255, ...) at most 64 rows name the same one
- gate_probs: bfloat16 [4096, 2], P(('dp', 'expert')), may hold values from 0.19921875 to 1
- w_gate: bfloat16 [4, 4096, 768], P('expert'), may hold values from -0.09375 to 0.09375
- w_up: bfloat16 [4, 4096, 768], P('expert'), may hold values from -0.09375 to 0.09375
- w_down: bfloat16 [4, 768, 4096], P('expert'), may hold values from -0.21875 to 0.21875
Outputs:
- x_grad: bfloat16 [4096, 4096], P(('dp', 'expert'))
- prob_grad: bfloat16 [4096, 2], P(('dp', 'expert'))
- gate_grad: float32 [4, 4096, 768], P('expert', 'dp')
- up_grad: float32 [4, 4096, 768], P('expert', 'dp')
- down_grad: float32 [4, 768, 4096], P('expert', None, 'dp')
The draws below stay inside these ranges and needn't reach their ends.
Inputs may be any that keep to these rules, and one draw needn't show every extreme that they name: `routes`: each token names 2 different experts; the 128 tokens of one device (aligned blocks of rows) name one expert at most 64 times, a bound that some block reaches.
All inputs are finite; a program needn't handle non-finite values.
Results may differ from the reference program's by a relative error of at most 0.013.
Values may be sent and summed in bfloat16 or wider, within the bound.
No kernel may reach another device: no remote copies, remote signals or barrier semaphores. Data moves between devices by JAX's collectives and lax.ppermute only.
A program may use at most 192 MiB of HBM per device.

```python
import math
import jax
import jax.numpy as jnp
import numpy as np
from jax import lax

D = 4096
FFW = 768
TOPW = 2
TOK_DEV = 128
CAP = 64
E = 4
REPLICAS = 8
GROUP_TOK = 512
TOKENS = 4096
N_EXPERT = 4


def shard_levels(stream_key, extent, cuts, low, largest):
    def one(axis_at, blocks):
        heights = jax.random.uniform(jax.random.fold_in(jax.random.fold_in(stream_key, 6), axis_at), (blocks,), jnp.float32, low / len(cuts), largest / len(cuts))
        return jnp.repeat(jnp.exp(heights), extent[axis_at] // blocks).reshape((-1,) + (1,) * (len(extent) - axis_at - 1))

    factor_of = one(*cuts[0])
    for cut in cuts[1:]:
        factor_of = factor_of * one(*cut)
    return factor_of


def deal_out(key, own, number, rows, amount, top, most, slope):
    ranking = jax.random.permutation(key, amount)
    heavy_load, ordinary = shares(amount, rows * top, most, slope, True), shares(amount, rows * top, most, slope, False)
    places = jnp.arange(amount)

    def named(sizes, offset_by):
        used = int((sizes > 0).sum())
        fixed = max(1, used // 4)
        passed = fixed + (places - fixed + offset_by * (used - fixed)) % max(1, amount - fixed)
        return jnp.zeros((amount,), jnp.int32).at[ranking[jnp.where(places < fixed, places, passed)]].set(jnp.asarray(sizes, jnp.int32))

    sizes = jnp.where(number % 4 == 0, named(heavy_load, number // 4), named(ordinary, number - number // 4 - 1))
    mixed = jax.random.permutation(jax.random.fold_in(own, 3), amount)
    giver, taker = mixed[0:amount // 2 * 2:2], mixed[1:amount // 2 * 2:2]
    margin = jnp.minimum(sizes[giver] - 1, most - sizes[taker]) // 2
    margin = jnp.where((giver == ranking[0]) | (taker == ranking[0]) | (sizes[taker] == 0), 0, jnp.maximum(margin, 0))
    passed = jax.random.randint(jax.random.fold_in(own, 4), (amount // 2,), 0, 1 << 20) % (margin + 1)
    sizes = sizes.at[giver].add(-passed).at[taker].add(passed)
    labels = jnp.searchsorted(jnp.cumsum(sizes), jnp.arange(rows * top), side="right").astype(jnp.int32)
    grid = labels.reshape(top, rows).T
    grid = grid[jax.random.permutation(jax.random.fold_in(own, 1), rows)]
    offset_by = jax.random.randint(jax.random.fold_in(own, 2), (rows, 1), 0, top)
    return jnp.take_along_axis(grid, (jnp.arange(top)[None, :] + offset_by) % top, axis=1)


def shares(amount, total, most, slope, full):
    portions = [(1 << 20) // math.isqrt(standing ** slope) + 1 for standing in range(1, amount + 1)]
    largest = most if full else min(most, max(-(-total // amount), total * portions[0] // sum(portions)))
    least = 1 if total - largest >= amount - 1 else 0
    counts, spare = [largest] + [least] * (amount - 1), total - largest - least * (amount - 1)
    while spare > 0:
        movable = [i for i in range(1, amount) if counts[i] < largest] or [i for i in range(1, amount) if counts[i] < most]
        pool, left = sum([portions[i] for i in movable]), spare
        for i in movable:
            more = min(most - counts[i], max(1, left * portions[i] // pool), spare)
            counts[i] = counts[i] + more
            spare = spare - more
    return np.array(counts)


def normal_values(key, shape, scale, limit, split=(), held_as=jnp.bfloat16):
    values = jax.random.normal(key, shape, jnp.float32) * scale
    if len(split) > 0:
        values = shard_levels(key, shape, split, -0.22, 0.18) * values
    return jnp.clip(values, min=-limit, max=limit).astype(held_as)


def setup_inputs(seed: int = 0) -> dict:
    splits = jax.random.split(jax.random.key(seed), 8)
    tokens = normal_values(splits[0], (TOKENS, D), 1.0, 6.0, ((0, 32),))
    out_grad = normal_values(splits[1], (TOKENS, D), 1.0, 6.0, ((0, 32),))
    routes_keys = jax.random.split(jax.random.fold_in(splits[2], 1), TOKENS // TOK_DEV)
    routes_turns = jax.random.permutation(jax.random.fold_in(splits[2], 3), TOKENS // TOK_DEV)
    routes = jax.vmap(lambda own, number: deal_out(jax.random.fold_in(splits[2], 2), own, number, TOK_DEV, E, TOPW, CAP, 2))(routes_keys, routes_turns).reshape((TOKENS, TOPW))
    gate_probs = jnp.clip(0.19921875 + 0.80078125 * jax.random.uniform(splits[3], (TOKENS, TOPW), jnp.float32) ** shard_levels(splits[3], (TOKENS, TOPW), ((0, 32),), -0.2, 0.2), 0.19921875, 1.0).astype(jnp.bfloat16)
    w_gate = normal_values(splits[4], (E, D, FFW), D ** -0.5, 0.09375, ((0, 4),))
    w_up = normal_values(splits[5], (E, D, FFW), D ** -0.5, 0.09375, ((0, 4),))
    w_down = normal_values(splits[6], (E, FFW, D), FFW ** -0.5, 0.21875, ((0, 4),))
    return {"tokens": tokens, "out_grad": out_grad, "routes": routes, "gate_probs": gate_probs, "w_gate": w_gate, "w_up": w_up, "w_down": w_down}


def expert_rows(x_group, g_group, flat_route, flat_prob, expert_id, w_gate, w_up, w_down):
    flat_total = GROUP_TOK * TOPW
    row_total = N_EXPERT * CAP
    sort_key = jnp.where(flat_route == expert_id, jnp.arange(flat_total, dtype=jnp.int32), flat_total)
    sorted_order = jnp.argsort(sort_key)[:row_total]
    picked = sort_key[sorted_order]
    is_valid = picked < flat_total
    source = jnp.minimum(picked, flat_total - 1).astype(jnp.int32)
    token_index = source // TOPW
    zero_value = jnp.zeros((), jnp.bfloat16)
    x_rows = jnp.where(is_valid[:, None], x_group[token_index], zero_value)
    g_rows = jnp.where(is_valid[:, None], g_group[token_index], zero_value)
    prob_rows = jnp.where(is_valid, flat_prob[source].astype(jnp.float32), jnp.zeros((), jnp.float32))
    gate_matrix = w_gate[expert_id]
    up_matrix = w_up[expert_id]
    down_matrix = w_down[expert_id]
    gate_pre = jnp.dot(x_rows, gate_matrix, preferred_element_type=jnp.float32)
    up_pre = jnp.dot(x_rows, up_matrix, preferred_element_type=jnp.float32)
    sigmoid_gate = jax.nn.sigmoid(gate_pre)
    activation = (gate_pre * sigmoid_gate * up_pre).astype(jnp.bfloat16)
    back_hidden = jnp.dot(g_rows, down_matrix.T, preferred_element_type=jnp.float32)
    hidden_grad = prob_rows[:, None] * back_hidden
    gate_delta = (hidden_grad * up_pre * sigmoid_gate * (1.0 + gate_pre * (1.0 - sigmoid_gate))).astype(jnp.bfloat16)
    up_delta = (hidden_grad * gate_pre * sigmoid_gate).astype(jnp.bfloat16)
    out_delta = (prob_rows[:, None] * g_rows.astype(jnp.float32)).astype(jnp.bfloat16)
    row_grad = (jnp.dot(gate_delta, gate_matrix.T, preferred_element_type=jnp.float32) + jnp.dot(up_delta, up_matrix.T, preferred_element_type=jnp.float32)).astype(jnp.bfloat16)
    outputs = jnp.dot(activation, down_matrix, preferred_element_type=jnp.float32)
    prob_rows_grad = lax.optimization_barrier(jnp.sum(g_rows.astype(jnp.float32) * outputs, axis=1)) / math.sqrt(D)
    grad_scale = 1.0 / math.sqrt(TOKENS)
    part_gate = (jnp.dot(x_rows.T, gate_delta, preferred_element_type=jnp.float32) * grad_scale).astype(jnp.bfloat16)
    part_up = (jnp.dot(x_rows.T, up_delta, preferred_element_type=jnp.float32) * grad_scale).astype(jnp.bfloat16)
    part_down = (jnp.dot(activation.T, out_delta, preferred_element_type=jnp.float32) * grad_scale).astype(jnp.bfloat16)
    return (part_gate, part_up, part_down, row_grad, prob_rows_grad, source, is_valid)

def reference(tokens, out_grad, routes, gate_probs, w_gate, w_up, w_down):
    flat_total = GROUP_TOK * TOPW
    x_all = tokens.reshape(REPLICAS, GROUP_TOK, D)
    g_all = out_grad.reshape(REPLICAS, GROUP_TOK, D)
    r_all = routes.reshape(REPLICAS, flat_total)
    p_all = gate_probs.reshape(REPLICAS, flat_total)

    def one_group(totals, operands):
        x_group, g_group, flat_route, flat_prob = operands

        def one_expert(expert_id):
            return expert_rows(x_group, g_group, flat_route, flat_prob, expert_id, w_gate, w_up, w_down)
        part_gate, part_up, part_down, row_grad, prob_rows_grad, source, is_valid = lax.map(one_expert, jnp.arange(E, dtype=jnp.int32))
        gate_sum, up_sum, down_sum = totals
        gate_sum = gate_sum + part_gate.astype(jnp.float32)
        up_sum = up_sum + part_up.astype(jnp.float32)
        down_sum = down_sum + part_down.astype(jnp.float32)
        valid_float = is_valid.astype(jnp.float32)
        token_index = (source // TOPW).reshape(-1)
        contrib = (row_grad.astype(jnp.float32) * valid_float[:, :, None]).reshape(-1, D)
        group_grad = jnp.zeros((GROUP_TOK, D), jnp.float32).at[token_index].add(contrib)
        slot_index = jnp.where(is_valid, source, flat_total).reshape(-1).astype(jnp.int32)
        group_prob = jnp.zeros((flat_total + 1,), jnp.float32).at[slot_index].set(prob_rows_grad.reshape(-1))
        return ((gate_sum, up_sum, down_sum), (group_grad.astype(jnp.bfloat16), group_prob[:flat_total].astype(jnp.bfloat16)))
    init = (jnp.zeros((E, D, FFW), jnp.float32), jnp.zeros((E, D, FFW), jnp.float32), jnp.zeros((E, FFW, D), jnp.float32))
    totals, per_group = lax.scan(one_group, init, (x_all, g_all, r_all, p_all))
    x_grad = per_group[0].reshape(TOKENS, D)
    prob_grad = per_group[1].reshape(TOKENS, TOPW)
    return (x_grad, prob_grad, totals[0], totals[1], totals[2])
```

```python
import functools
import math

import jax
import jax.numpy as jnp
from jax import lax
from jax.experimental import pallas as pl
from jax.experimental.pallas import tpu as pltpu
from jax.sharding import PartitionSpec as P

CAP = 64
CHUNKS = 2
EXTRA = 128
F32 = jnp.float32
BF16 = jnp.bfloat16
VMEM_LIMIT = 48 * 1024 * 1024


def whole(shape):
    return pl.BlockSpec(shape, lambda i, pos: (0,) * len(shape))


def call(kernel, grid, in_specs, out_specs, out_shape, pos, args, flops=0, scratch=()):
    moved = sum(a.size * a.dtype.itemsize for a in args)
    moved += sum(math.prod(o.shape) * o.dtype.itemsize for o in jax.tree.leaves(out_shape))
    return pl.pallas_call(
        kernel,
        grid_spec=pltpu.PrefetchScalarGridSpec(
            num_scalar_prefetch=1,
            grid=grid,
            in_specs=in_specs,
            out_specs=out_specs,
            scratch_shapes=list(scratch),
        ),
        out_shape=out_shape,
        compiler_params=pltpu.CompilerParams(vmem_limit_bytes=VMEM_LIMIT),
        cost_estimate=pl.CostEstimate(flops=flops, bytes_accessed=moved, transcendentals=0),
    )(pos, *args)


def shape_of(shape, dtype=BF16):
    return jax.ShapeDtypeStruct(shape, dtype)


def dot(left, right):
    return jnp.dot(left, right, preferred_element_type=F32)


def dot_t(left, right):
    return lax.dot_general(left, right, (((1,), (1,)), ((), ())), preferred_element_type=F32)


def shard_at(i, me, replicas):
    half = replicas // 2
    return jnp.where(i < half, 2 * i + 1, 2 * i - replicas) ^ me


def slot_expert(rows, cols, my_expert):
    return (lax.broadcasted_iota(jnp.int32, (rows, cols), 1) // CAP) ^ my_expert


def slot_matrix(routes_ref, my_expert, slots):
    tok = routes_ref.shape[0]
    expert = slot_expert(tok, slots, my_expert)
    hit = jnp.zeros((tok, slots), jnp.bool_)
    for k in range(routes_ref.shape[1]):
        hit = hit | (routes_ref[:, k : k + 1] == expert)
    named = jnp.where(hit, 1.0, 0.0)
    before = lax.broadcasted_iota(jnp.int32, (tok, tok), 1) < lax.broadcasted_iota(
        jnp.int32, (tok, tok), 0
    )
    rank = dot(jnp.where(before, 1.0, 0.0).astype(BF16), named.astype(BF16))
    place = (lax.broadcasted_iota(jnp.int32, (tok, slots), 1) % CAP).astype(F32)
    return jnp.where(rank == place, named, 0.0), expert


def send_tokens_kernel(experts, pos_ref, routes_ref, tok_ref, *rest):
    outs, place_ref, pt_ref = rest[:experts], rest[experts], rest[experts + 1]

    @pl.when(pl.program_id(0) == 0)
    def _():
        place, _ = slot_matrix(routes_ref, pos_ref[1], experts * CAP)
        place_ref[...] = place.astype(BF16)
        pt_ref[...] = place.T.astype(BF16)

    rows = dot(pt_ref[...], tok_ref[...]).astype(BF16)
    for j in range(experts):
        outs[j][...] = rows[j * CAP : (j + 1) * CAP]


def send_cot_kernel(experts, pos_ref, routes_ref, probs_ref, cot_ref, dep_ref, *rest):
    outs, pt_ref = rest[:experts], rest[experts]

    @pl.when(pl.program_id(0) == 0)
    def _():
        place, expert = slot_matrix(routes_ref, pos_ref[1], experts * CAP)
        probs = probs_ref[...].astype(F32)
        weight = jnp.zeros_like(place)
        for k in range(routes_ref.shape[1]):
            weight += jnp.where(routes_ref[:, k : k + 1] == expert, probs[:, k : k + 1], 0.0)
        pt_ref[...] = (place * weight).T.astype(BF16)

    rows = dot(pt_ref[...], cot_ref[...]).astype(BF16)
    for j in range(experts):
        outs[j][...] = rows[j * CAP : (j + 1) * CAP]


def forward_kernel(experts, replicas, pos_ref, *rest):
    xs, (wg_ref, wu_ref), outs, x_ref = (
        rest[:experts],
        rest[experts : experts + 2],
        rest[experts + 2 : -1],
        rest[-1],
    )
    act_ref, act_t_ref, for_gate_ref, for_up_ref = outs

    @pl.when(pl.program_id(0) == 0)
    def _():
        for j in range(experts):
            x_ref[j * CAP : (j + 1) * CAP, :] = xs[j][...]

    width = wg_ref.shape[1] // replicas
    gate = jnp.zeros(act_ref.shape, F32)
    up = jnp.zeros(act_ref.shape, F32)
    for i in range(replicas):
        at = pl.ds(pl.multiple_of(shard_at(i, pos_ref[0], replicas) * width, width), width)
        part = x_ref[:, i * width : (i + 1) * width]
        gate += dot(part, wg_ref[0, at, :])
        up += dot(part, wu_ref[0, at, :])
    sig = jax.nn.sigmoid(gate)
    silu = gate * sig
    act = silu * up
    act_ref[...] = act.astype(BF16)
    act_t_ref[...] = act.T.astype(BF16)
    for_gate_ref[...] = up * sig * (1.0 + gate * (1.0 - sig))
    for_up_ref[...] = silu


def transpose_kernel(experts, pos_ref, *rest):
    rows = jnp.concatenate([ref[...] for ref in rest[:experts]], axis=0)
    rest[experts][...] = rows.T


def down_far_kernel(experts, scale, pos_ref, act_t_ref, *rest):
    rows = jnp.concatenate([ref[...] for ref in rest[:experts]], axis=0)
    rest[experts][...] = (dot(act_t_ref[...], rows) * scale).astype(BF16)


def scatter_pieces(part, q, outs):
    low_send, low_keep, high_send, high_keep = outs
    pieces = pl.num_programs(0)
    half = part.shape[0] // 2

    @pl.when(q % 2 == 1)
    def _():
        low_send[0] = part[:half].astype(BF16)

    @pl.when(q % 2 == 0)
    def _():
        low_keep[0] = part[:half]

    @pl.when(q >= pieces // 2)
    def _():
        high_send[0] = part[half:].astype(BF16)

    @pl.when(q < pieces // 2)
    def _():
        high_keep[0] = part[half:]


def scatter_specs(pieces, rows, cols):
    block = (1, rows // 2, cols)
    half = pieces // 2
    specs = [
        pl.BlockSpec(block, lambda q, pos: (q // 2, 0, 0)),
        pl.BlockSpec(block, lambda q, pos: (q // 2, 0, 0)),
        pl.BlockSpec(block, lambda q, pos: (jnp.maximum(q - half, 0), 0, 0)),
        pl.BlockSpec(block, lambda q, pos: (jnp.minimum(q, half - 1), 0, 0)),
    ]
    shapes = [shape_of((half, rows // 2, cols), t) for t in (BF16, F32, BF16, F32)]
    return specs, shapes


def down_near_kernel(experts, scale, pos_ref, act_t_ref, other_ref, *rest):
    rows = jnp.concatenate([ref[...] for ref in rest[:experts]], axis=0)
    part = dot(act_t_ref[...], rows) * scale + other_ref[...].astype(F32)
    scatter_pieces(part, pl.program_id(0), rest[experts:])


def back_hidden_kernel(experts, last, pos_ref, wd_ref, *rest):
    i = pl.program_id(0)
    rows = jnp.concatenate([ref[...] for ref in rest[:experts]], axis=0)
    rest = rest[experts:]
    if last:
        prev_ref, act_ref, for_gate_ref, for_up_ref, dh_ref, du_ref, prob_ref, sum_ref = rest
    else:
        (sum_ref,) = rest
    term = dot_t(rows, wd_ref[0])

    @pl.when(i == 0)
    def _():
        sum_ref[...] = term + prev_ref[...] if last else term

    @pl.when(i > 0)
    def _():
        sum_ref[...] += term

    if last:

        @pl.when(i == pl.num_programs(0) - 1)
        def _():
            back = sum_ref[...]
            dh_ref[...] = (back * for_gate_ref[...]).astype(BF16)
            du_ref[...] = (back * for_up_ref[...]).astype(BF16)
            prob_ref[...] = jnp.sum(act_ref[...].astype(F32) * back, axis=1, keepdims=True)


def grad_far_kernel(scale, pos_ref, xt_ref, delta_ref, out_ref):
    out_ref[...] = (dot(xt_ref[...], delta_ref[...]) * scale).astype(BF16)


def grad_near_kernel(scale, pos_ref, xt_ref, delta_ref, other_ref, *outs):
    part = dot(xt_ref[...], delta_ref[...]) * scale + other_ref[...].astype(F32)
    scatter_pieces(part, pl.program_id(0), outs)


def row_grad_kernel(experts, pos_ref, dh_ref, du_ref, prob_ref, wg_ref, wu_ref, *outs):
    i = pl.program_id(0)
    width = wg_ref.shape[1]
    rows = (dot_t(dh_ref[...], wg_ref[0]) + dot_t(du_ref[...], wu_ref[0])).astype(BF16)
    at = pl.ds(pl.multiple_of(i * width, width), width)
    for j in range(experts):
        outs[j][:, at] = rows[j * CAP : (j + 1) * CAP]

    @pl.when(i == 0)
    def _():
        full = prob_ref[...]
        high = full.astype(BF16).astype(F32)
        lane = lax.broadcasted_iota(jnp.int32, (full.shape[0], EXTRA), 1)
        both = jnp.where(lane == 0, high, jnp.where(lane == 1, full - high, 0.0)).astype(BF16)
        for j in range(experts):
            outs[j][:, outs[j].shape[1] - EXTRA :] = both[j * CAP : (j + 1) * CAP]


def combine_kernel(experts, scale, pos_ref, place_ref, routes_ref, probs_ref, *rest):
    backs, extras = rest[:experts], rest[experts : 2 * experts]
    x_ref, prob_ref = rest[2 * experts :]
    rows = jnp.concatenate([ref[...] for ref in backs], axis=0)
    x_ref[...] = dot(place_ref[...], rows).astype(BF16)

    @pl.when(pl.program_id(0) == 0)
    def _():
        place = place_ref[...].astype(F32)
        extra = jnp.concatenate([ref[...] for ref in extras], axis=0)
        expert = slot_expert(place.shape[0], place.shape[1], pos_ref[1])
        probs = probs_ref[...].astype(F32)
        lane = lax.broadcasted_iota(jnp.int32, probs.shape, 1)
        result = jnp.zeros(probs.shape, F32)
        for k in range(routes_ref.shape[1]):
            mine = jnp.where(routes_ref[:, k : k + 1] == expert, place, 0.0).astype(BF16)
            found = jnp.sum(dot(mine, extra), axis=1, keepdims=True)
            result += jnp.where(lane == k, found, 0.0)
        prob_ref[...] = (result * scale / probs).astype(BF16)


def flip(x, axis, bit):
    count = lax.axis_size(axis)
    return lax.ppermute(x, axis, [(i, i ^ bit) for i in range(count)])


def halve(send, keep, bits, low):
    for at, bit in enumerate(bits):
        total = keep + flip(send, "dp", bit).astype(F32)
        if at + 1 == len(bits):
            return total[0]
        if low:
            pairs = total.reshape(total.shape[0] // 2, 2, *total.shape[1:])
            send, keep = pairs[:, 1].astype(BF16), pairs[:, 0]
        else:
            half = total.shape[0] // 2
            send, keep = total[half:].astype(BF16), total[:half]


def body(tokens, out_grad, routes, gate_probs, w_gate, w_up, w_down):
    tok, width = tokens.shape
    experts = lax.axis_size("expert")
    replicas = lax.axis_size("dp")
    hidden = w_gate.shape[2]
    slots = experts * CAP
    shard = width // replicas
    pieces = replicas // 2
    grad_scale = 1.0 / math.sqrt(tok * replicas * experts)
    prob_scale = 1.0 / math.sqrt(width)
    pos = jnp.stack([lax.axis_index("dp"), lax.axis_index("expert")]).astype(jnp.int32)
    bits = [1 << (b + 1) for b in range(pieces.bit_length() - 1)]

    def exchange(blocks):
        return [blocks[0]] + [flip(blocks[j], "expert", j) for j in range(experts - 1, 0, -1)][::-1]

    def block_specs(cols, at):
        return [pl.BlockSpec((CAP, cols), at) for _ in range(experts)]

    *x_out, place = call(
        functools.partial(send_tokens_kernel, experts),
        (replicas,),
        [
            whole(routes.shape),
            pl.BlockSpec((tok, shard), lambda i, pos: (0, shard_at(i, pos[0], replicas))),
        ],
        block_specs(shard, lambda i, pos: (0, i)) + [whole((tok, slots))],
        [shape_of((CAP, width)) for _ in range(experts)] + [shape_of((tok, slots))],
        pos,
        [routes, tokens],
        flops=2 * tok * slots * width,
        scratch=[pltpu.VMEM((slots, tok), BF16)],
    )
    x_in = exchange(x_out)

    part = shard // CHUNKS
    cols = width // CHUNKS

    def send_cot(c, dep):
        out = call(
            functools.partial(send_cot_kernel, experts),
            (replicas,),
            [
                whole(routes.shape),
                whole(gate_probs.shape),
                pl.BlockSpec(
                    (tok, part), lambda i, pos: (0, shard_at(i, pos[0], replicas) * CHUNKS + c)
                ),
                pl.BlockSpec(memory_space=pl.ANY),
            ],
            block_specs(part, lambda i, pos: (0, i)),
            [shape_of((CAP, cols)) for _ in range(experts)],
            pos,
            [routes, gate_probs, out_grad, dep],
            flops=2 * tok * slots * cols,
            scratch=[pltpu.VMEM((slots, tok), BF16)],
        )
        return exchange(out)

    dy = [send_cot(0, place)]
    for c in range(1, CHUNKS):
        dy.append(send_cot(c, dy[c - 1][1] if c > 1 else x_in[1]))

    hid = hidden // 3
    act, act_t, for_gate, for_up = call(
        functools.partial(forward_kernel, experts, replicas),
        (3,),
        [whole((CAP, width)) for _ in range(experts)]
        + [pl.BlockSpec((1, width, hid), lambda i, pos: (0, 0, i)) for _ in range(2)],
        [
            pl.BlockSpec((slots, hid), lambda i, pos: (0, i)),
            pl.BlockSpec((hid, slots), lambda i, pos: (i, 0)),
            pl.BlockSpec((slots, hid), lambda i, pos: (0, i)),
            pl.BlockSpec((slots, hid), lambda i, pos: (0, i)),
        ],
        [
            shape_of((slots, hidden)),
            shape_of((hidden, slots)),
            shape_of((slots, hidden), F32),
            shape_of((slots, hidden), F32),
        ],
        pos,
        [*x_in, w_gate, w_up],
        flops=4 * slots * width * hidden,
        scratch=[pltpu.VMEM((slots, width), BF16)],
    )
    (x_t,) = call(
        functools.partial(transpose_kernel, experts),
        (replicas,),
        block_specs(shard, lambda i, pos: (0, i)),
        [pl.BlockSpec((shard, slots), lambda i, pos: (i, 0))],
        [shape_of((width, slots))],
        pos,
        x_in,
    )

    down_parts = []
    back = None
    for c in range(CHUNKS):
        (far,) = call(
            functools.partial(down_far_kernel, experts, grad_scale),
            (pieces,),
            [whole((hidden, slots))] + block_specs(part, lambda i, pos: (0, i)),
            [pl.BlockSpec((hidden, part), lambda i, pos: (0, i))],
            [shape_of((hidden, pieces * part))],
            pos,
            [act_t, *dy[c]],
            flops=hidden * slots * cols,
        )
        other = flip(far, "dp", 1)
        last = c + 1 == CHUNKS
        specs = [
            pl.BlockSpec(
                (1, hidden, part),
                lambda i, pos, c=c: (0, 0, shard_at(i, pos[0], replicas) * CHUNKS + c),
            )
        ] + block_specs(part, lambda i, pos: (0, i))
        full = whole((slots, hidden))
        if last:
            dh, du, prob = call(
                functools.partial(back_hidden_kernel, experts, True),
                (replicas,),
                specs + [full] * 4,
                [full, full, whole((slots, 1))],
                [
                    shape_of((slots, hidden)),
                    shape_of((slots, hidden)),
                    shape_of((slots, 1), F32),
                ],
                pos,
                [w_down, *dy[c], back, act, for_gate, for_up],
                flops=2 * slots * hidden * cols,
                scratch=[pltpu.VMEM((slots, hidden), F32)],
            )
        else:
            (back,) = call(
                functools.partial(back_hidden_kernel, experts, False),
                (replicas,),
                specs,
                [full],
                [shape_of((slots, hidden), F32)],
                pos,
                [w_down, *dy[c]],
                flops=2 * slots * hidden * cols,
            )
        out_specs, out_shapes = scatter_specs(pieces, hidden, part)
        low_send, low_keep, high_send, high_keep = call(
            functools.partial(down_near_kernel, experts, grad_scale),
            (pieces,),
            [whole((hidden, slots)), pl.BlockSpec((hidden, part), lambda i, pos: (0, i))]
            + block_specs(part, lambda i, pos: (0, i + pieces)),
            out_specs,
            out_shapes,
            pos,
            [act_t, other, *dy[c]],
            flops=hidden * slots * cols,
        )
        low = halve(low_send, low_keep, bits, True)
        high = halve(high_send, high_keep, bits[::-1], False)
        down_parts.append(jnp.concatenate([low, high], axis=0))
    down_grad = jnp.concatenate(down_parts, axis=1)[None]

    fars = []
    for delta in (dh, du):
        (far,) = call(
            functools.partial(grad_far_kernel, grad_scale),
            (pieces,),
            [pl.BlockSpec((shard, slots), lambda i, pos: (i, 0)), whole((slots, hidden))],
            [pl.BlockSpec((shard, hidden), lambda i, pos: (i, 0))],
            [shape_of((pieces * shard, hidden))],
            pos,
            [x_t, delta],
            flops=width * slots * hidden,
        )
        fars.append(flip(far, "dp", 1))

    back_out = call(
        functools.partial(row_grad_kernel, experts),
        (8,),
        [whole((slots, hidden)), whole((slots, hidden)), whole((slots, 1))]
        + [pl.BlockSpec((1, width // 8, hidden), lambda i, pos: (0, i, 0)) for _ in range(2)],
        [whole((CAP, width + EXTRA)) for _ in range(experts)],
        [shape_of((CAP, width + EXTRA)) for _ in range(experts)],
        pos,
        [dh, du, prob, w_gate, w_up],
        flops=4 * slots * width * hidden,
    )
    back_in = exchange(back_out)

    grads = []
    for delta, other in zip((dh, du), fars):
        out_specs, out_shapes = scatter_specs(pieces, shard, hidden)
        low_send, low_keep, high_send, high_keep = call(
            functools.partial(grad_near_kernel, grad_scale),
            (pieces,),
            [
                pl.BlockSpec((shard, slots), lambda i, pos: (i + pieces, 0)),
                whole((slots, hidden)),
                pl.BlockSpec((shard, hidden), lambda i, pos: (i, 0)),
            ],
            out_specs,
            out_shapes,
            pos,
            [x_t, delta, other],
            flops=width * slots * hidden,
        )
        low = halve(low_send, low_keep, bits, True)
        high = halve(high_send, high_keep, bits[::-1], False)
        grads.append(jnp.concatenate([low, high], axis=0)[None])

    step = width // 8
    x_grad, prob_grad = call(
        functools.partial(combine_kernel, experts, prob_scale),
        (8,),
        [whole((tok, slots)), whole(routes.shape), whole(gate_probs.shape)]
        + block_specs(step, lambda i, pos: (0, i))
        + block_specs(EXTRA, lambda i, pos: (0, width // EXTRA)),
        [pl.BlockSpec((tok, step), lambda i, pos: (0, i)), whole(gate_probs.shape)],
        [shape_of((tok, width)), shape_of(gate_probs.shape)],
        pos,
        [place, routes, gate_probs, *back_in, *back_in],
        flops=2 * tok * slots * width,
    )
    return (x_grad, prob_grad, grads[0], grads[1], down_grad)


def solution(mesh):
    return jax.shard_map(
        body,
        mesh=mesh,
        in_specs=(
            P(("dp", "expert"), None),
            P(("dp", "expert"), None),
            P(("dp", "expert"), None),
            P(("dp", "expert"), None),
            P("expert", None, None),
            P("expert", None, None),
            P("expert", None, None),
        ),
        out_specs=(
            P(("dp", "expert"), None),
            P(("dp", "expert"), None),
            P("expert", "dp", None),
            P("expert", "dp", None),
            P("expert", None, "dp"),
        ),
        check_vma=False,
    )
```

```python
import functools
import math

import jax
import jax.numpy as jnp
from jax import lax
from jax.experimental import pallas as pl
from jax.experimental.pallas import tpu as pltpu
from jax.sharding import PartitionSpec as P

CAP = 64
EXTRA = 128
F32 = jnp.float32
BF16 = jnp.bfloat16
LONG = 10**12
VMEM_SPARE = 6 * 1024 * 1024


def whole(shape):
    return pl.BlockSpec(shape, lambda i, pos: (0,) * len(shape))


def call(kernel, grid, in_specs, out_specs, out_shape, pos, args, after, scratch=(), cost=1):
    held = sum(math.prod(ref.shape) * ref.dtype.itemsize for ref in scratch)
    for spec, array in zip([*in_specs, *out_specs], [*args, *out_shape]):
        if spec.block_shape is not None:
            held += 2 * math.prod(spec.block_shape) * array.dtype.itemsize
    first, count = 1 + len(args), len(after)

    def ordered(*refs):
        kernel(*refs[:first], *refs[first + count :])

    return pl.pallas_call(
        ordered,
        grid_spec=pltpu.PrefetchScalarGridSpec(
            num_scalar_prefetch=1,
            grid=grid,
            in_specs=list(in_specs) + [pl.BlockSpec(memory_space=pl.ANY)] * count,
            out_specs=out_specs,
            scratch_shapes=list(scratch),
        ),
        out_shape=out_shape,
        compiler_params=pltpu.CompilerParams(vmem_limit_bytes=held + VMEM_SPARE),
        cost_estimate=pl.CostEstimate(flops=cost, bytes_accessed=1, transcendentals=0),
    )(pos, *args, *after)


def shape_of(shape, dtype=BF16):
    return jax.ShapeDtypeStruct(shape, dtype)


def dot(left, right):
    return jnp.dot(left, right, preferred_element_type=F32)


def shard_at(i, me, replicas):
    half = replicas // 2
    return jnp.where(i < half, 2 * i + 1, 2 * i - replicas) ^ me


def slot_expert(rows, cols, my_expert):
    return (lax.broadcasted_iota(jnp.int32, (rows, cols), 1) // CAP) ^ my_expert


def slot_matrix(routes_ref, my_expert, slots):
    tok = routes_ref.shape[0]
    expert = slot_expert(tok, slots, my_expert)
    hit = jnp.zeros((tok, slots), jnp.bool_)
    for k in range(routes_ref.shape[1]):
        hit = hit | (routes_ref[:, k : k + 1] == expert)
    named = jnp.where(hit, 1.0, 0.0)
    before = lax.broadcasted_iota(jnp.int32, (tok, tok), 1) < lax.broadcasted_iota(
        jnp.int32, (tok, tok), 0
    )
    rank = dot(jnp.where(before, 1.0, 0.0).astype(BF16), named.astype(BF16))
    place = (lax.broadcasted_iota(jnp.int32, (tok, slots), 1) % CAP).astype(F32)
    return jnp.where(rank == place, named, 0.0), expert


def send_tokens_kernel(experts, replicas, pos_ref, routes_ref, tok_ref, *rest):
    outs, place_ref = rest[:experts], rest[experts]
    place, _ = slot_matrix(routes_ref, pos_ref[1], experts * CAP)
    place_ref[...] = place.astype(BF16)
    place_t = place.T.astype(BF16)
    width = tok_ref.shape[1] // replicas
    for i in range(replicas):
        at = pl.ds(pl.multiple_of(shard_at(i, pos_ref[0], replicas) * width, width), width)
        rows = dot(place_t, tok_ref[:, at]).astype(BF16)
        for j in range(experts):
            outs[j][:, i * width : (i + 1) * width] = rows[j * CAP : (j + 1) * CAP]


def send_cot_kernel(experts, replicas, pos_ref, routes_ref, probs_ref, cot_ref, *outs):
    place, expert = slot_matrix(routes_ref, pos_ref[1], experts * CAP)
    probs = probs_ref[...].astype(F32)
    weight = jnp.zeros_like(place)
    for k in range(routes_ref.shape[1]):
        weight += jnp.where(routes_ref[:, k : k + 1] == expert, probs[:, k : k + 1], 0.0)
    weighted = (place * weight).T.astype(BF16)
    width = cot_ref.shape[1] // replicas
    for i in range(replicas):
        at = pl.ds(pl.multiple_of(shard_at(i, pos_ref[0], replicas) * width, width), width)
        rows = dot(weighted, cot_ref[:, at]).astype(BF16)
        for j in range(experts):
            outs[j][:, i * width : (i + 1) * width] = rows[j * CAP : (j + 1) * CAP]


def forward_kernel(experts, replicas, pos_ref, *rest):
    xs, (wg_ref, wu_ref), outs, x_ref = (
        rest[:experts],
        rest[experts : experts + 2],
        rest[experts + 2 : -1],
        rest[-1],
    )
    act_ref, act_t_ref, for_gate_ref, for_up_ref = outs

    @pl.when(pl.program_id(0) == 0)
    def _():
        for j in range(experts):
            x_ref[j * CAP : (j + 1) * CAP, :] = xs[j][...]

    width = wg_ref.shape[1] // replicas
    gate = jnp.zeros(act_ref.shape, F32)
    up = jnp.zeros(act_ref.shape, F32)
    for i in range(replicas):
        at = pl.ds(pl.multiple_of(shard_at(i, pos_ref[0], replicas) * width, width), width)
        part = x_ref[:, i * width : (i + 1) * width]
        gate += dot(part, wg_ref[0, at, :])
        up += dot(part, wu_ref[0, at, :])
    gate, up = gate.T, up.T
    sig = jax.nn.sigmoid(gate)
    silu = gate * sig
    act = (silu * up).astype(BF16)
    act_ref[...] = act.T
    act_t_ref[...] = act
    for_gate_ref[...] = up * sig * (1.0 + gate * (1.0 - sig))
    for_up_ref[...] = silu


def joined(refs):
    return jnp.concatenate([ref[...] for ref in refs], axis=0)


def transpose_kernel(pos_ref, *rest):
    rest[-1][...] = joined(rest[:-1]).T


def scatter_pieces(part, q, outs):
    low_send, low_keep, high_send, high_keep = outs
    pieces = pl.num_programs(0)
    half = part.shape[0] // 2

    @pl.when(q % 2 == 1)
    def _():
        low_send[0] = part[:half].astype(BF16)

    @pl.when(q % 2 == 0)
    def _():
        low_keep[0] = part[:half]

    @pl.when(q >= pieces // 2)
    def _():
        high_send[0] = part[half:].astype(BF16)

    @pl.when(q < pieces // 2)
    def _():
        high_keep[0] = part[half:]


def scatter_specs(pieces, rows, cols):
    block = (1, rows // 2, cols)
    half = pieces // 2
    specs = [
        pl.BlockSpec(block, lambda q, pos: (q // 2, 0, 0)),
        pl.BlockSpec(block, lambda q, pos: (q // 2, 0, 0)),
        pl.BlockSpec(block, lambda q, pos: (jnp.maximum(q - half, 0), 0, 0)),
        pl.BlockSpec(block, lambda q, pos: (jnp.minimum(q, half - 1), 0, 0)),
    ]
    shapes = [shape_of((half, rows // 2, cols), t) for t in (BF16, F32, BF16, F32)]
    return specs, shapes


def back_hidden_kernel(
    pos_ref,
    wd_ref,
    dyt_ref,
    act_ref,
    for_gate_ref,
    for_up_ref,
    delta_ref,
    delta_t_ref,
    prob_ref,
    sum_ref,
):
    i = pl.program_id(0)
    term = dot(wd_ref[0], dyt_ref[...])

    @pl.when(i == 0)
    def _():
        sum_ref[...] = term

    @pl.when(i > 0)
    def _():
        sum_ref[...] += term

    @pl.when(i == pl.num_programs(0) - 1)
    def _():
        back = sum_ref[...]
        dh = (back * for_gate_ref[...]).astype(BF16)
        du = (back * for_up_ref[...]).astype(BF16)
        hidden = back.shape[0]
        delta_t_ref[:hidden] = dh
        delta_t_ref[hidden:] = du
        delta_ref[:, :hidden] = dh.T
        delta_ref[:, hidden:] = du.T
        prob_ref[...] = jnp.sum(act_ref[...].astype(F32) * back, axis=0, keepdims=True)


def grad_far_kernel(scale, pos_ref, xt_ref, delta_ref, out_ref):
    out_ref[...] = (dot(xt_ref[...], delta_ref[...]) * scale).astype(BF16)


def grad_near_kernel(scale, pos_ref, xt_ref, delta_ref, *rest):
    others, outs = rest[:-4], rest[-4:]
    other = jnp.concatenate([ref[...] for ref in others], axis=1)
    part = dot(xt_ref[...], delta_ref[...]) * scale + other.astype(F32)
    scatter_pieces(part, pl.program_id(0), outs)


def row_grad_kernel(pos_ref, delta_t_ref, prob_ref, wg_ref, wu_ref, *outs):
    i = pl.program_id(0)
    width, hidden = wg_ref.shape[1:]
    rows_t = dot(wg_ref[0], delta_t_ref[:hidden]) + dot(wu_ref[0], delta_t_ref[hidden:])
    rows = rows_t.astype(BF16).T
    at = pl.ds(pl.multiple_of(i * width, width), width)
    for j, out_ref in enumerate(outs):
        out_ref[:, at] = rows[j * CAP : (j + 1) * CAP]

    @pl.when(i == 0)
    def _():
        full = prob_ref[...]
        high = full.astype(BF16).astype(F32)
        lane = lax.broadcasted_iota(jnp.int32, (EXTRA, full.shape[1]), 0)
        both = jnp.where(lane == 0, high, jnp.where(lane == 1, full - high, 0.0)).T.astype(BF16)
        for j, out_ref in enumerate(outs):
            out_ref[:, out_ref.shape[1] - EXTRA :] = both[j * CAP : (j + 1) * CAP]


def add_kernel(pos_ref, *rest):
    ins, outs = rest[:-4], rest[-4:]

    def total(first):
        pairs = [(ins[k], ins[k + 1]) for k in range(first, len(ins), 4)]
        return jnp.concatenate([keep[0] + came[0].astype(F32) for keep, came in pairs], axis=1)

    part = jnp.concatenate([total(0), total(2)], axis=0)
    scatter_pieces(part, pl.program_id(0), outs)


def mark_kernel(pos_ref, out_ref):
    out_ref[...] = jnp.zeros(out_ref.shape, F32)


def combine_kernel(scale, pos_ref, place_ref, routes_ref, probs_ref, *rest):
    experts = (len(rest) - 2) // 2
    x_ref, prob_ref = rest[2 * experts :]
    rows = joined(rest[:experts])
    x_ref[...] = dot(place_ref[...], rows).astype(BF16)

    @pl.when(pl.program_id(0) == 0)
    def _():
        place = place_ref[...].astype(F32)
        extra = joined(rest[experts : 2 * experts])
        expert = slot_expert(place.shape[0], place.shape[1], pos_ref[1])
        probs = probs_ref[...].astype(F32)
        lane = lax.broadcasted_iota(jnp.int32, probs.shape, 1)
        result = jnp.zeros(probs.shape, F32)
        for k in range(routes_ref.shape[1]):
            mine = jnp.where(routes_ref[:, k : k + 1] == expert, place, 0.0).astype(BF16)
            found = jnp.sum(dot(mine, extra), axis=1, keepdims=True)
            result += jnp.where(lane == k, found, 0.0)
        prob_ref[...] = (result * scale / probs).astype(BF16)


def finish_kernel(
    pos_ref, low_keep_ref, low_ref, high_keep_ref, high_ref, down_ref, gate_ref, up_ref
):
    cols = gate_ref.shape[1]

    def total(keep_ref, ref, at):
        part = slice(at * cols, (at + 1) * cols)
        return keep_ref[0, :, part] + ref[0, :, part].astype(F32)

    halves = ((low_keep_ref, low_ref), (high_keep_ref, high_ref))
    down_ref[...] = jnp.concatenate([total(*half, 0).T for half in halves], axis=1)
    for at, out_ref in ((1, gate_ref), (2, up_ref)):
        out_ref[...] = jnp.concatenate([total(*half, at) for half in halves], axis=0)


def flip(x, axis, bit):
    count = lax.axis_size(axis)
    return lax.ppermute(x, axis, [(i, i ^ bit) for i in range(count)])


def body(tokens, out_grad, routes, gate_probs, w_gate, w_up, w_down):
    tok, width = tokens.shape
    experts = lax.axis_size("expert")
    replicas = lax.axis_size("dp")
    hidden = w_gate.shape[2]
    slots = experts * CAP
    shard = width // replicas
    pieces = replicas // 2
    levels = pieces.bit_length() - 1
    grad_scale = 1.0 / math.sqrt(tok * replicas * experts)
    prob_scale = 1.0 / math.sqrt(width)
    pos = jnp.stack([lax.axis_index("dp"), lax.axis_index("expert")]).astype(jnp.int32)
    chain = []

    def run(kernel, grid, in_specs, out_specs, out_shape, args, after=(), **kw):
        out = call(
            kernel, grid, in_specs, out_specs, out_shape, pos, args, [*chain[-1:], *after], **kw
        )
        chain.append(out[0])
        return out

    def exchange(blocks):
        return [blocks[0]] + [flip(blocks[j], "expert", j) for j in range(experts - 1, 0, -1)][::-1]

    def block_specs(cols, at):
        return [pl.BlockSpec((CAP, cols), at) for _ in range(experts)]

    def cross(state, level):
        low_send, low_keep, high_send, high_keep = state
        return (
            low_keep,
            flip(low_send, "dp", 2 << level),
            high_keep,
            flip(high_send, "dp", 2 << (levels - 1 - level)),
        )

    def add(*states):
        count, rows = states[0][0].shape[:2]
        specs, shapes = scatter_specs(count, 2 * rows, sum(s[0].shape[2] for s in states))
        ins = [a for state in states for a in state]
        blocks = [pl.BlockSpec((1, *a.shape[1:]), lambda q, pos: (q, 0, 0)) for a in ins]
        return run(add_kernel, (count,), blocks, specs, shapes, ins)

    def mark(after, cost):
        run(mark_kernel, (1,), [], [whole((8, 128))], [shape_of((8, 128), F32)], [], after, cost=cost)

    blocks = [whole((CAP, width)) for _ in range(experts)]
    *x_out, place = run(
        functools.partial(send_tokens_kernel, experts, replicas),
        (1,),
        [whole(routes.shape), whole(tokens.shape)],
        [*blocks, whole((tok, slots))],
        [shape_of((CAP, width)) for _ in range(experts)] + [shape_of((tok, slots))],
        [routes, tokens],
    )
    x_in = exchange(x_out)

    dy_out = run(
        functools.partial(send_cot_kernel, experts, replicas),
        (1,),
        [whole(routes.shape), whole(gate_probs.shape), whole(out_grad.shape)],
        blocks,
        [shape_of((CAP, width)) for _ in range(experts)],
        [routes, gate_probs, out_grad],
        [x_in[1]],
    )
    dy = exchange(dy_out)

    def grad_far(rows_t, right, which):
        (far,) = run(
            functools.partial(grad_far_kernel, grad_scale),
            (pieces,),
            [
                pl.BlockSpec((shard, slots), lambda i, pos: (i, 0)),
                pl.BlockSpec((slots, hidden), lambda i, pos: (0, which)),
            ],
            [pl.BlockSpec((shard, hidden), lambda i, pos: (i, 0))],
            [shape_of((pieces * shard, hidden))],
            [rows_t, right],
        )
        return flip(far, "dp", 1)

    def grad_near(rows_t, right, others):
        specs, shapes = scatter_specs(pieces, shard, right.shape[1])
        return run(
            functools.partial(grad_near_kernel, grad_scale),
            (pieces,),
            [
                pl.BlockSpec((shard, slots), lambda i, pos: (i + pieces, 0)),
                whole(right.shape),
            ]
            + [pl.BlockSpec((shard, hidden), lambda i, pos: (i, 0))] * len(others),
            specs,
            shapes,
            [rows_t, right, *others],
        )

    def transpose(rows):
        (out,) = run(
            transpose_kernel,
            (replicas,),
            block_specs(shard, lambda i, pos: (0, i)),
            [pl.BlockSpec((shard, slots), lambda i, pos: (i, 0))],
            [shape_of((width, slots))],
            rows,
        )
        return out

    hid = hidden // 3
    act, act_t, for_gate, for_up = run(
        functools.partial(forward_kernel, experts, replicas),
        (3,),
        [whole((CAP, width)) for _ in range(experts)]
        + [pl.BlockSpec((1, width, hid), lambda i, pos: (0, 0, i)) for _ in range(2)],
        [pl.BlockSpec((slots, hid), lambda i, pos: (0, i))]
        + [pl.BlockSpec((hid, slots), lambda i, pos: (i, 0))] * 3,
        [shape_of((slots, hidden))] + [shape_of((hidden, slots), t) for t in (BF16, F32, F32)],
        [*x_in, w_gate, w_up],
        scratch=[pltpu.VMEM((slots, width), BF16)],
    )
    x_t = transpose(x_in)
    dy_t = transpose(dy)

    other = grad_far(dy_t, act, 0)
    delta, delta_t, prob = run(
        back_hidden_kernel,
        (replicas,),
        [
            pl.BlockSpec(
                (1, hidden, shard), lambda i, pos: (0, 0, shard_at(i, pos[0], replicas))
            ),
            pl.BlockSpec((shard, slots), lambda i, pos: (i, 0)),
        ]
        + [whole((hidden, slots))] * 3,
        [whole((slots, 2 * hidden)), whole((2 * hidden, slots)), whole((1, slots))],
        [
            shape_of((slots, 2 * hidden)),
            shape_of((2 * hidden, slots)),
            shape_of((1, slots), F32),
        ],
        [w_down, dy_t, act_t, for_gate, for_up],
        scratch=[pltpu.VMEM((hidden, slots), F32)],
    )
    down = cross(grad_near(dy_t, act, [other]), 0)
    others = [grad_far(x_t, delta, 0), grad_far(x_t, delta, 1)]

    back_out = run(
        row_grad_kernel,
        (8,),
        [whole((2 * hidden, slots)), whole((1, slots))]
        + [pl.BlockSpec((1, width // 8, hidden), lambda i, pos: (0, i, 0)) for _ in range(2)],
        [whole((CAP, width + EXTRA)) for _ in range(experts)],
        [shape_of((CAP, width + EXTRA)) for _ in range(experts)],
        [delta_t, prob, w_gate, w_up],
    )
    back_in = exchange(back_out)

    both = cross(grad_near(x_t, delta, others), 0)
    mark([down[1], down[3]], 1)
    mark([], LONG)
    state = add(down, both)
    for level in range(1, levels):
        state = cross(state, level)
        if level + 1 < levels:
            state = add(state)

    step = width // 4
    x_grad, prob_grad = run(
        functools.partial(combine_kernel, prob_scale),
        (4,),
        [whole((tok, slots)), whole(routes.shape), whole(gate_probs.shape)]
        + block_specs(step, lambda i, pos: (0, i))
        + block_specs(EXTRA, lambda i, pos: (0, width // EXTRA)),
        [pl.BlockSpec((tok, step), lambda i, pos: (0, i)), whole(gate_probs.shape)],
        [shape_of((tok, width)), shape_of(gate_probs.shape)],
        [place, routes, gate_probs, *back_in, *back_in],
        cost=LONG,
    )
    down_grad, gate_grad, up_grad = run(
        finish_kernel,
        (1,),
        [whole(state[0].shape)] * 4,
        [whole((hidden, shard)), whole((shard, hidden)), whole((shard, hidden))],
        [shape_of((hidden, shard), F32)] + [shape_of((shard, hidden), F32)] * 2,
        state,
    )
    return (x_grad, prob_grad, gate_grad[None], up_grad[None], down_grad[None])


def solution(mesh):
    return jax.shard_map(
        body,
        mesh=mesh,
        in_specs=(
            P(("dp", "expert"), None),
            P(("dp", "expert"), None),
            P(("dp", "expert"), None),
            P(("dp", "expert"), None),
            P("expert", None, None),
            P("expert", None, None),
            P("expert", None, None),
        ),
        out_specs=(
            P(("dp", "expert"), None),
            P(("dp", "expert"), None),
            P("expert", "dp", None),
            P("expert", "dp", None),
            P("expert", None, "dp"),
        ),
        check_vma=False,
    )
```

```python
import functools
import math

import jax
import jax.numpy as jnp
from jax import lax
from jax.experimental import pallas as pl
from jax.experimental.pallas import tpu as pltpu
from jax.sharding import PartitionSpec as P

CAP = 64
EXTRA = 128
F32 = jnp.float32
BF16 = jnp.bfloat16
LONG = 6 * 10**10
VMEM_SPARE = 2 * 1024 * 1024


def whole(shape):
    return pl.BlockSpec(shape, lambda i, pos: (0,) * len(shape))


def call(kernel, grid, in_specs, out_specs, out_shape, pos, args, after, scratch=(), cost=1):
    held = sum(math.prod(ref.shape) * ref.dtype.itemsize for ref in scratch)
    for spec, array in zip([*in_specs, *out_specs], [*args, *out_shape]):
        if spec.block_shape is not None:
            held += 2 * math.prod(spec.block_shape) * array.dtype.itemsize
    first, count, last = 1 + len(args), len(after), len(out_shape)

    def ordered(*refs):
        outs = refs[first + count :]
        kernel(*refs[:first], *outs[:last], *outs[last + 1 :])
        outs[last][...] = jnp.zeros(outs[last].shape, F32)

    return pl.pallas_call(
        ordered,
        grid_spec=pltpu.PrefetchScalarGridSpec(
            num_scalar_prefetch=1,
            grid=grid,
            in_specs=list(in_specs) + [pl.BlockSpec(memory_space=pl.ANY)] * count,
            out_specs=[*out_specs, whole((8, 128))],
            scratch_shapes=list(scratch),
        ),
        out_shape=[*out_shape, shape_of((8, 128), F32)],
        compiler_params=pltpu.CompilerParams(vmem_limit_bytes=held + VMEM_SPARE),
        cost_estimate=pl.CostEstimate(flops=cost, bytes_accessed=1, transcendentals=0),
    )(pos, *args, *after)


def shape_of(shape, dtype=BF16):
    return jax.ShapeDtypeStruct(shape, dtype)


def dot(left, right):
    return jnp.dot(left, right, preferred_element_type=F32)


def shard_at(i, me, replicas):
    half = replicas // 2
    return jnp.where(i < half, 2 * i + 1, 2 * i - replicas) ^ me


def slot_matrix(routes_ref, my_expert, slots):
    top, tok = routes_ref.shape
    index = lax.broadcasted_iota(jnp.int32, (slots, tok), 0)
    expert = (index // CAP) ^ my_expert
    hit = jnp.zeros((slots, tok), jnp.bool_)
    for k in range(top):
        hit = hit | (routes_ref[k : k + 1, :] == expert)
    named = jnp.where(hit, 1.0, 0.0)
    before = lax.broadcasted_iota(jnp.int32, (tok, tok), 0) < lax.broadcasted_iota(
        jnp.int32, (tok, tok), 1
    )
    rank = dot(named.astype(BF16), jnp.where(before, 1.0, 0.0).astype(BF16))
    return jnp.where(rank == (index % CAP).astype(F32), named, 0.0), expert


def send_tokens_kernel(experts, replicas, pos_ref, routes_ref, tok_ref, *outs):
    place, _ = slot_matrix(routes_ref, pos_ref[1], experts * CAP)
    place = place.astype(BF16)
    width = tok_ref.shape[1] // replicas
    for i in range(replicas):
        at = pl.ds(pl.multiple_of(shard_at(i, pos_ref[0], replicas) * width, width), width)
        rows = dot(place, tok_ref[:, at]).astype(BF16)
        for j in range(experts):
            outs[j][:, i * width : (i + 1) * width] = rows[j * CAP : (j + 1) * CAP]


def send_cot_kernel(
    experts, replicas, pos_ref, routes_ref, probs_ref, cot_ref, *rest
):
    outs, place_t_ref = rest[:-1], rest[-1]
    place, expert = slot_matrix(routes_ref, pos_ref[1], experts * CAP)
    probs = probs_ref[...].astype(F32)
    weight = jnp.zeros_like(place)
    for k in range(routes_ref.shape[0]):
        weight += jnp.where(routes_ref[k : k + 1, :] == expert, probs[k : k + 1, :], 0.0)
    weighted = (place * weight).astype(BF16)
    width = cot_ref.shape[1] // replicas
    for i in range(replicas):
        at = pl.ds(pl.multiple_of(shard_at(i, pos_ref[0], replicas) * width, width), width)
        rows = dot(weighted, cot_ref[:, at]).astype(BF16)
        for j in range(experts):
            outs[j][:, i * width : (i + 1) * width] = rows[j * CAP : (j + 1) * CAP]
    place_t_ref[...] = place.T.astype(BF16)


def forward_kernel(experts, replicas, pos_ref, *rest):
    xs, (wg_ref, wu_ref), outs, x_ref = (
        rest[:experts],
        rest[experts : experts + 2],
        rest[experts + 2 : -1],
        rest[-1],
    )
    act_ref, act_t_ref, for_gate_ref, for_up_ref = outs

    @pl.when(pl.program_id(0) == 0)
    def _():
        for j in range(experts):
            x_ref[j * CAP : (j + 1) * CAP, :] = xs[j][...]

    width = wg_ref.shape[1] // replicas
    gate = jnp.zeros(act_ref.shape, F32)
    up = jnp.zeros(act_ref.shape, F32)
    for i in range(replicas):
        at = pl.ds(pl.multiple_of(shard_at(i, pos_ref[0], replicas) * width, width), width)
        part = x_ref[:, i * width : (i + 1) * width]
        gate += dot(part, wg_ref[0, at, :])
        up += dot(part, wu_ref[0, at, :])
    gate, up = gate.T, up.T
    sig = jax.nn.sigmoid(gate)
    silu = gate * sig
    act = (silu * up).astype(BF16)
    act_ref[...] = act.T
    act_t_ref[...] = act
    for_gate_ref[...] = up * sig * (1.0 + gate * (1.0 - sig))
    for_up_ref[...] = silu


def joined(refs):
    return jnp.concatenate([ref[...] for ref in refs], axis=0)


def transpose_kernel(pos_ref, *rest):
    rest[-1][...] = joined(rest[:-1]).T


def transpose_far_kernel(scale, pos_ref, act_ref, *rest):
    ins, (far_t_ref, near_t_ref, far_ref) = rest[:-3], rest[-3:]
    middle = len(ins) // 2
    rows_t = joined(ins[:middle]).T
    far_t_ref[...] = rows_t
    far_ref[...] = (dot(rows_t, act_ref[...]) * scale).astype(BF16)
    near_t_ref[...] = joined(ins[middle:]).T


def back_hidden_kernel(pos_ref, *rest):
    weights, rest = rest[:4], rest[4:]
    far_t_ref, near_t_ref, act_ref, for_gate_ref, for_up_ref, *outs, sum_ref = rest
    delta_ref, delta_t_ref, prob_ref = outs
    i = pl.program_id(0)
    width = weights[0].shape[2]
    term = sum(
        dot(weights[at][0], ref[at % 2 * width : (at % 2 + 1) * width])
        for at, ref in enumerate((far_t_ref, far_t_ref, near_t_ref, near_t_ref))
    )

    @pl.when(i == 0)
    def _():
        sum_ref[...] = term

    @pl.when(i > 0)
    def _():
        sum_ref[...] += term

    @pl.when(i == pl.num_programs(0) - 1)
    def _():
        back = sum_ref[...]
        dh = (back * for_gate_ref[...]).astype(BF16)
        du = (back * for_up_ref[...]).astype(BF16)
        hidden = back.shape[0]
        delta_t_ref[:hidden] = dh
        delta_t_ref[hidden:] = du
        delta_ref[:, :hidden] = dh.T
        delta_ref[:, hidden:] = du.T
        prob_ref[...] = jnp.sum(act_ref[...].astype(F32) * back, axis=0, keepdims=True)


def grad_far_kernel(scale, pos_ref, xt_ref, delta_ref, *outs):
    part = (dot(xt_ref[...], delta_ref[...]) * scale).astype(BF16)
    cols = outs[0].shape[1]
    for at, out_ref in enumerate(outs):
        out_ref[...] = part[:, at * cols : (at + 1) * cols]


def grad_near_kernel(scale, pos_ref, xt_ref, delta_ref, *rest):
    others, (low_send, low_keep, high_send, high_keep) = rest[:-4], rest[-4:]
    hidden = others[0].shape[1]
    rows = xt_ref.shape[0] // 2
    half = rows // 2
    first = pl.program_id(0) < pl.num_programs(0) // 2

    def upper(out_ref, piece, at, part):
        out_ref[piece, at * half : (at + 1) * half] = part

    for at, ref in enumerate(others):
        part = dot(xt_ref[...], delta_ref[:, at * hidden : (at + 1) * hidden]) * scale
        part = (part + ref[...].astype(F32)).astype(BF16)
        low_keep[0, at * half : (at + 1) * half] = part[:half]
        low_send[0, at * half : (at + 1) * half] = part[rows : rows + half]
        for piece in (0, 1):
            high = part[piece * rows + half : (piece + 1) * rows]
            pl.when(first)(functools.partial(upper, high_keep, piece, at, high))
            pl.when(jnp.logical_not(first))(functools.partial(upper, high_send, piece, at, high))


def row_grad_kernel(pos_ref, delta_t_ref, prob_ref, wg_ref, wu_ref, *outs):
    i = pl.program_id(0)
    width, hidden = wg_ref.shape[1:]
    rows_t = dot(wg_ref[0], delta_t_ref[:hidden]) + dot(wu_ref[0], delta_t_ref[hidden:])
    rows = rows_t.astype(BF16).T
    at = pl.ds(pl.multiple_of(i * width, width), width)
    for j, out_ref in enumerate(outs):
        out_ref[:, at] = rows[j * CAP : (j + 1) * CAP]

    @pl.when(i == 0)
    def _():
        full = prob_ref[...]
        high = full.astype(BF16).astype(F32)
        lane = lax.broadcasted_iota(jnp.int32, (EXTRA, full.shape[1]), 0)
        both = jnp.where(lane == 0, high, jnp.where(lane == 1, full - high, 0.0)).T.astype(BF16)
        for j, out_ref in enumerate(outs):
            out_ref[:, out_ref.shape[1] - EXTRA :] = both[j * CAP : (j + 1) * CAP]


def total_of(refs):
    down, *rest = [ref[0].astype(F32) for ref in refs]
    first = [down, rest[0] + rest[1], rest[2] + rest[3]]
    return sum(rest[4:], jnp.concatenate(first, axis=0))


def add_kernel(pos_ref, *rest):
    ins, outs = rest[:-2], rest[-2:]
    middle = len(ins) // 2
    for refs, out_ref in zip((ins[:middle], ins[middle:]), outs):
        out_ref[0] = total_of(refs).astype(BF16)


def add_pairs_kernel(pos_ref, a_ref, b_ref, c_ref, d_ref, low_ref, high_ref):
    low_ref[...] = (a_ref[...].astype(F32) + b_ref[...].astype(F32)).astype(BF16)
    high_ref[...] = (c_ref[...].astype(F32) + d_ref[...].astype(F32)).astype(BF16)


def combine_kernel(scale, pos_ref, place_ref, routes_ref, probs_ref, *rest):
    experts = (len(rest) - 2) // 2
    x_ref, prob_ref = rest[2 * experts :]
    rows = joined(rest[:experts])
    x_ref[...] = dot(place_ref[...], rows).astype(BF16)

    @pl.when(pl.program_id(0) == 0)
    def _():
        extra = joined(rest[experts : 2 * experts])
        tok, slots = place_ref.shape
        top = routes_ref.shape[0]
        place, expert = slot_matrix(routes_ref, pos_ref[1], slots)
        value = jnp.sum(extra.astype(F32), axis=1, keepdims=True)
        probs = probs_ref[...].astype(F32)
        line = lax.broadcasted_iota(jnp.int32, probs.shape, 0)
        result = jnp.zeros(probs.shape, F32)
        for k in range(top):
            mine = jnp.where(routes_ref[k : k + 1, :] == expert, place, 0.0)
            found = jnp.sum(mine * value, axis=0, keepdims=True)
            result += jnp.where(line == k, found, 0.0)
        prob_ref[...] = (result * scale / probs).astype(BF16)


def finish_kernel(
    pos_ref, low_ref, low_last_ref, high_ref, high_last_ref, down_ref, gate_ref, up_ref
):
    rows = gate_ref.shape[0]
    lower = pl.program_id(0) < pl.num_programs(0) // 2

    def write(ref, last_ref):
        total = ref[0].astype(F32) + last_ref[0].astype(F32)
        down_ref[...] = total[:rows].T
        gate_ref[...] = total[rows : 2 * rows]
        up_ref[...] = total[2 * rows :]

    @pl.when(lower)
    def _():
        write(low_ref, low_last_ref)

    @pl.when(jnp.logical_not(lower))
    def _():
        write(high_ref, high_last_ref)


def flip(x, axis, bit):
    count = lax.axis_size(axis)
    return lax.ppermute(x, axis, [(i, i ^ bit) for i in range(count)])


def body(tokens, out_grad, routes, gate_probs, w_gate, w_up, w_down):
    tok, width = tokens.shape
    experts = lax.axis_size("expert")
    replicas = lax.axis_size("dp")
    hidden = w_gate.shape[2]
    slots = experts * CAP
    shard = width // replicas
    pieces = replicas // 2
    levels = pieces.bit_length() - 1
    grad_scale = 1.0 / math.sqrt(tok * replicas * experts)
    prob_scale = 1.0 / math.sqrt(width)
    pos = jnp.stack([lax.axis_index("dp"), lax.axis_index("expert")]).astype(jnp.int32)
    chain = []

    def run(kernel, grid, in_specs, out_specs, out_shape, args, after=(), **kw):
        out = call(
            kernel, grid, in_specs, out_specs, out_shape, pos, args, [*chain[-1:], *after], **kw
        )
        chain.append(out[-1])
        return out[:-1]

    def exchange(blocks):
        return [blocks[0]] + [flip(blocks[j], "expert", j) for j in range(experts - 1, 0, -1)][::-1]

    def block_specs(cols, at):
        return [pl.BlockSpec((CAP, cols), at) for _ in range(experts)]

    def cross(low, high, level):
        return flip(low, "dp", 2 << level), flip(high, "dp", 2 << (levels - 1 - level))

    half = shard // 2
    steps, rows = 1, half

    def add(halves, level, count, places):
        specs, arrays = [], []
        for high, (down, keep, came, *later) in enumerate(halves):

            def spec(size, first, behind, high=high):
                shift = 0 if high else behind
                return pl.BlockSpec(
                    (1, size, hidden),
                    lambda i, pos: (places[high](i // steps) << shift, first + i % steps, 0),
                )

            specs += [spec(rows, at, level - 1) for at in (0, 0, 0, steps, steps)]
            arrays += [down, keep, came, keep, came]
            for at, array in enumerate(later):
                specs.append(spec(3 * rows, 0, level - 2 - at))
                arrays.append(array)
        return run(
            add_kernel,
            (count * steps,),
            specs,
            [pl.BlockSpec((1, 3 * rows, hidden), lambda i, pos: (i // steps, i % steps, 0))] * 2,
            [shape_of((count, 3 * half, hidden))] * 2,
            arrays,
        )

    def mark(after, cost):
        run(lambda pos_ref: None, (1,), [], [], [], [], after, cost=cost)

    blocks = [whole((CAP, width)) for _ in range(experts)]
    routes, gate_probs = routes.T, gate_probs.T
    x_out = run(
        functools.partial(send_tokens_kernel, experts, replicas),
        (1,),
        [whole(routes.shape), whole(tokens.shape)],
        blocks,
        [shape_of((CAP, width)) for _ in range(experts)],
        [routes, tokens],
    )
    x_in = exchange(x_out)

    *dy_out, place = run(
        functools.partial(send_cot_kernel, experts, replicas),
        (1,),
        [whole(routes.shape), whole(gate_probs.shape), whole(out_grad.shape)],
        [*blocks, whole((tok, slots))],
        [shape_of((CAP, width)) for _ in range(experts)] + [shape_of((tok, slots))],
        [routes, gate_probs, out_grad],
        [x_in[1]],
    )
    dy = exchange(dy_out)

    def grad_near(rows_t, first, right, others):
        size = half * len(others)
        grid = pieces // 2
        return run(
            functools.partial(grad_near_kernel, grad_scale),
            (grid,),
            [
                pl.BlockSpec((2 * shard, slots), lambda i, pos: (i + first, 0)),
                whole(right.shape),
            ]
            + [pl.BlockSpec((2 * shard, hidden), lambda i, pos: (i, 0))] * len(others),
            [pl.BlockSpec((1, size, hidden), lambda i, pos: (i, 0, 0))] * 2
            + [
                pl.BlockSpec(
                    (2, size, hidden), lambda i, pos: (jnp.maximum(i - grid // 2, 0), 0, 0)
                ),
                pl.BlockSpec(
                    (2, size, hidden), lambda i, pos: (jnp.minimum(i, grid // 2 - 1), 0, 0)
                ),
            ],
            [shape_of((grid, size, hidden))] * 4,
            [rows_t, right, *others],
        )

    hid = hidden // 3
    act, act_t, for_gate, for_up = run(
        functools.partial(forward_kernel, experts, replicas),
        (3,),
        [whole((CAP, width)) for _ in range(experts)]
        + [pl.BlockSpec((1, width, hid), lambda i, pos: (0, 0, i)) for _ in range(2)],
        [pl.BlockSpec((slots, hid), lambda i, pos: (0, i))]
        + [pl.BlockSpec((hid, slots), lambda i, pos: (i, 0))] * 3,
        [shape_of((slots, hidden))] + [shape_of((hidden, slots), t) for t in (BF16, F32, F32)],
        [*x_in, w_gate, w_up],
        scratch=[pltpu.VMEM((slots, width), BF16)],
    )
    (x_t,) = run(
        transpose_kernel,
        (4,),
        block_specs(width // 4, lambda i, pos: (0, i)),
        [pl.BlockSpec((width // 4, slots), lambda i, pos: (i, 0))],
        [shape_of((width, slots))],
        x_in,
    )
    far_t, near_t, far = run(
        functools.partial(transpose_far_kernel, grad_scale),
        (2,),
        [whole((slots, hidden))]
        + block_specs(width // 4, lambda i, pos: (0, i))
        + block_specs(width // 4, lambda i, pos: (0, i + 2)),
        [pl.BlockSpec((width // 4, slots), lambda i, pos: (i, 0))] * 2
        + [pl.BlockSpec((width // 4, hidden), lambda i, pos: (i, 0))],
        [shape_of((width // 2, slots))] * 2 + [shape_of((width // 2, hidden))],
        [act, *dy, *dy],
    )
    other = flip(far, "dp", 1)
    delta, delta_t, prob = run(
        back_hidden_kernel,
        (replicas // 4,),
        [
            pl.BlockSpec(
                (1, hidden, shard),
                lambda i, pos, at=at: (0, 0, shard_at(2 * i + at, pos[0], replicas)),
            )
            for at in (0, 1, pieces, pieces + 1)
        ]
        + [pl.BlockSpec((2 * shard, slots), lambda i, pos: (i, 0))] * 2
        + [whole((hidden, slots))] * 3,
        [whole((slots, 2 * hidden)), whole((2 * hidden, slots)), whole((1, slots))],
        [
            shape_of((slots, 2 * hidden)),
            shape_of((2 * hidden, slots)),
            shape_of((1, slots), F32),
        ],
        [w_down] * 4 + [far_t, near_t, act_t, for_gate, for_up],
        scratch=[pltpu.VMEM((hidden, slots), F32)],
    )
    far = run(
        functools.partial(grad_far_kernel, grad_scale),
        (2,),
        [pl.BlockSpec((width // 4, slots), lambda i, pos: (i, 0)), whole((slots, 2 * hidden))],
        [pl.BlockSpec((width // 4, hidden), lambda i, pos: (i, 0))] * 2,
        [shape_of((width // 2, hidden))] * 2,
        [x_t, delta],
    )
    others = [flip(part, "dp", 1) for part in far]
    low_send, low_keep, high_send, high_keep = grad_near(near_t, 0, act, [other])
    down_low, down_high = cross(low_send, high_send, 0)
    down_keep = low_keep, high_keep

    back_out = run(
        row_grad_kernel,
        (4,),
        [whole((2 * hidden, slots)), whole((1, slots))]
        + [pl.BlockSpec((1, width // 4, hidden), lambda i, pos: (0, i, 0)) for _ in range(2)],
        [whole((CAP, width + EXTRA)) for _ in range(experts)],
        [shape_of((CAP, width + EXTRA)) for _ in range(experts)],
        [delta_t, prob, w_gate, w_up],
    )
    back_in = exchange(back_out)

    low_send, low_keep, high_send, high_keep = grad_near(x_t, pieces // 2, delta, others)
    low, high = cross(low_send, high_send, 0)
    down_low, down_high = run(
        add_pairs_kernel,
        (1,),
        [whole(low_keep.shape[:1] + (half, hidden))] * 4,
        [whole(low_keep.shape[:1] + (half, hidden))] * 2,
        [shape_of(low_keep.shape[:1] + (half, hidden))] * 2,
        [down_keep[0], down_low, down_keep[1], down_high],
    )
    mark([], LONG)
    halves = [[down_low, low_keep, low], [down_high, high_keep, high]]
    for level in range(1, levels):
        count = pieces >> (level + 1)
        places = lambda i: 2 * i + 1, lambda i, count=count: count + i
        low, high = cross(*add(halves, level, count, places), level)
        if level + 1 < levels:
            halves[0].append(low)
            halves[1].append(high)
    mine = add(halves, levels, 1, (lambda i: i, lambda i: i))

    step = width // 2
    x_grad, prob_grad = run(
        functools.partial(combine_kernel, prob_scale),
        (2,),
        [whole((tok, slots)), whole(routes.shape), whole(gate_probs.shape)]
        + block_specs(step, lambda i, pos: (0, i))
        + block_specs(EXTRA, lambda i, pos: (0, width // EXTRA)),
        [pl.BlockSpec((tok, step), lambda i, pos: (0, i)), whole(gate_probs.shape)],
        [shape_of((tok, width)), shape_of(gate_probs.shape)],
        [place, routes, gate_probs, *back_in, *back_in],
        cost=LONG,
    )
    low_spec = pl.BlockSpec(
        (1, 3 * rows, hidden), lambda i, pos: (0, jnp.minimum(i, steps - 1), 0)
    )
    high_spec = pl.BlockSpec(
        (1, 3 * rows, hidden), lambda i, pos: (0, jnp.maximum(i - steps, 0), 0)
    )
    down_grad, gate_grad, up_grad = run(
        finish_kernel,
        (2 * steps,),
        [low_spec, low_spec, high_spec, high_spec],
        [pl.BlockSpec((hidden, rows), lambda i, pos: (0, i))]
        + [pl.BlockSpec((rows, hidden), lambda i, pos: (i, 0))] * 2,
        [shape_of((hidden, shard), F32)] + [shape_of((shard, hidden), F32)] * 2,
        [mine[0], low, mine[1], high],
    )
    return (x_grad, prob_grad.T, gate_grad[None], up_grad[None], down_grad[None])


def solution(mesh):
    return jax.shard_map(
        body,
        mesh=mesh,
        in_specs=(
            P(("dp", "expert"), None),
            P(("dp", "expert"), None),
            P(("dp", "expert"), None),
            P(("dp", "expert"), None),
            P("expert", None, None),
            P("expert", None, None),
            P("expert", None, None),
        ),
        out_specs=(
            P(("dp", "expert"), None),
            P(("dp", "expert"), None),
            P("expert", "dp", None),
            P("expert", "dp", None),
            P("expert", None, "dp"),
        ),
        check_vma=False,
    )
```

```python
import functools
import math

import jax
import jax.numpy as jnp
from jax import lax
from jax.experimental import pallas as pl
from jax.experimental.pallas import tpu as pltpu
from jax.sharding import PartitionSpec as P

CAP = 64
FIRST = 128
EXTRA = 128
F32 = jnp.float32
BF16 = jnp.bfloat16
LONG = 6 * 10**10
VMEM_SPARE = 4 * 1024 * 1024


IN_VMEM = pl.BlockSpec(memory_space=pltpu.VMEM)


def whole(shape):
    return pl.BlockSpec(shape, lambda i, pos: (0,) * len(shape))


def call(kernel, grid, in_specs, out_specs, out_shape, pos, args, after, scratch=(), cost=1):
    held = sum(math.prod(ref.shape) * ref.dtype.itemsize for ref in scratch)
    for spec, array in zip([*in_specs, *out_specs], [*args, *out_shape]):
        if spec.block_shape is not None:
            held += 2 * math.prod(spec.block_shape) * array.dtype.itemsize
    first, count, last = 1 + len(args), len(after), len(out_shape)

    def ordered(*refs):
        outs = refs[first + count :]
        kernel(*refs[:first], *outs[:last], *outs[last + 1 :])
        outs[last][...] = jnp.zeros(outs[last].shape, F32)

    return pl.pallas_call(
        ordered,
        grid_spec=pltpu.PrefetchScalarGridSpec(
            num_scalar_prefetch=1,
            grid=grid,
            in_specs=list(in_specs) + [pl.BlockSpec(memory_space=pl.ANY)] * count,
            out_specs=[*out_specs, whole((8, 128))],
            scratch_shapes=list(scratch),
        ),
        out_shape=[*out_shape, shape_of((8, 128), F32)],
        compiler_params=pltpu.CompilerParams(vmem_limit_bytes=held + VMEM_SPARE),
        cost_estimate=pl.CostEstimate(flops=cost, bytes_accessed=1, transcendentals=0),
    )(pos, *args, *after)


def shape_of(shape, dtype=BF16):
    return jax.ShapeDtypeStruct(shape, dtype)


def dot(left, right):
    return jnp.dot(left, right, preferred_element_type=F32)


def shard_rows(relative, pos_ref, size):
    return pl.ds(pl.multiple_of((pos_ref[0] ^ relative) * size, size), size)


def slot_matrix(routes_ref, my_expert, slots):
    top, tok = routes_ref.shape
    index = lax.broadcasted_iota(jnp.int32, (slots, tok), 0)
    block = index // CAP
    expert = jnp.where(block == 0, 0, slots // CAP - block) ^ my_expert
    hit = jnp.zeros((slots, tok), jnp.bool_)
    for k in range(top):
        hit = hit | (routes_ref[k : k + 1, :] == expert)
    named = jnp.where(hit, 1.0, 0.0)
    before = lax.broadcasted_iota(jnp.int32, (tok, tok), 0) < lax.broadcasted_iota(
        jnp.int32, (tok, tok), 1
    )
    rank = dot(named.astype(BF16), jnp.where(before, 1.0, 0.0).astype(BF16))
    return jnp.where(rank == (index % CAP).astype(F32), named, 0.0), expert


def send_rows(place, ref, start, shard, outs):
    size = outs[0].shape[1] * shard // ref.shape[1]
    for i in range(ref.shape[1] // shard):
        rows = dot(place, ref[:, i * shard + start : i * shard + start + size]).astype(BF16)
        for j, out_ref in enumerate(outs):
            out_ref[:, i * size : (i + 1) * size] = rows[j * CAP : (j + 1) * CAP]


def send_tokens_kernel(shard, pos_ref, routes_ref, tok_ref, *outs):
    place, _ = slot_matrix(routes_ref, pos_ref[1], len(outs) * CAP)
    send_rows(place.astype(BF16), tok_ref, 0, shard, outs)


def send_cot_kernel(experts, shard, start, pos_ref, routes_ref, probs_ref, cot_ref, *rest):
    outs, place_t_ref = rest[:experts], rest[experts:]
    place, expert = slot_matrix(routes_ref, pos_ref[1], experts * CAP)
    probs = probs_ref[...].astype(F32)
    weight = jnp.zeros_like(place)
    for k in range(routes_ref.shape[0]):
        weight += jnp.where(routes_ref[k : k + 1, :] == expert, probs[k : k + 1, :], 0.0)
    send_rows((place * weight).astype(BF16), cot_ref, start, shard, outs)
    if place_t_ref:
        place_t_ref[0][...] = place.T.astype(BF16)


def joined(refs):
    return jnp.concatenate([ref[...] for ref in refs], axis=0)


def forward_kernel(experts, blocks, pos_ref, *rest):
    xs, (wg_ref, wu_ref), outs, x_ref = (
        rest[:experts],
        rest[experts : experts + 2],
        rest[experts + 2 : -1],
        rest[-1],
    )
    act_ref, act_t_ref, for_gate_ref, for_up_ref = outs
    for j in range(experts):
        x_ref[j * CAP : (j + 1) * CAP, :] = xs[j][...]
    size = wg_ref.shape[2] // blocks
    for i in range(blocks):
        at = slice(i * size, (i + 1) * size)
        gate = dot(x_ref[...], wg_ref[0, :, at]).T
        up = dot(x_ref[...], wu_ref[0, :, at]).T
        sig = jax.nn.sigmoid(gate)
        silu = gate * sig
        act = (silu * up).astype(BF16)
        act_ref[:, at] = act.T
        act_t_ref[at] = act
        for_gate_ref[at] = up * sig * (1.0 + gate * (1.0 - sig))
        for_up_ref[at] = silu


def transpose_kernel(pos_ref, *rest):
    ins, out_ref = rest[:-1], rest[-1]
    size = 512
    for at in range(0, out_ref.shape[0], size):
        rows = [ref[:, at : at + size] for ref in ins]
        out_ref[at : at + size] = jnp.concatenate(rows, axis=0).T


def grad_far_kernel(scale, replicas, pos_ref, rows_ref, right_ref, *outs):
    size = rows_ref.shape[0] // replicas
    cols = outs[0].shape[1]
    for i in range(replicas // 2):
        rows = rows_ref[shard_rows(2 * i + 1, pos_ref, size), :]
        part = (dot(rows, right_ref[...]) * scale).astype(BF16)
        for at, out_ref in enumerate(outs):
            out_ref[i * size : (i + 1) * size] = part[:, at * cols : (at + 1) * cols]


def grad_near_kernel(scale, replicas, pos_ref, rows_ref, right_ref, *rest):
    others, (low_send, low_keep, high_send, high_keep) = rest[:-4], rest[-4:]
    size = rows_ref.shape[0] // replicas
    cols = low_keep.shape[2]
    half, count = size // 2, replicas // 4
    for q in range(replicas // 2):
        rows = rows_ref[shard_rows(2 * q, pos_ref, size), :]
        low_ref = low_send if q % 2 else low_keep
        high_ref, place = (high_send, q - count) if q >= count else (high_keep, q)
        came = [ref[q * size : (q + 1) * size] for ref in others]
        came = jnp.concatenate(came, axis=1).astype(F32)
        total = (dot(rows, right_ref[...]) * scale + came).astype(BF16)
        for at in range(total.shape[1] // cols):
            part = total[:, at * cols : (at + 1) * cols]
            low_ref[q // 2, at * half : (at + 1) * half] = part[:half]
            high_ref[place, at * half : (at + 1) * half] = part[half:]


def back_sum(wd_ref, rows_ref, start, shard):
    count = wd_ref.shape[2] // shard
    size = rows_ref.shape[0] // count
    return sum(
        dot(
            wd_ref[0, :, i * shard + start : i * shard + start + size],
            rows_ref[i * size : (i + 1) * size],
        )
        for i in range(count)
    )


def back_first_kernel(shard, pos_ref, wd_ref, rows_ref, out_ref):
    out_ref[...] = back_sum(wd_ref, rows_ref, 0, shard)


def back_hidden_kernel(
    shard,
    pos_ref,
    prev_ref,
    wd_ref,
    rows_ref,
    act_ref,
    for_gate_ref,
    for_up_ref,
    delta_ref,
    delta_t_ref,
    prob_ref,
):
    back = prev_ref[...] + back_sum(wd_ref, rows_ref, FIRST, shard)
    dh = (back * for_gate_ref[...]).astype(BF16)
    du = (back * for_up_ref[...]).astype(BF16)
    hidden = back.shape[0]
    delta_t_ref[:hidden] = dh
    delta_t_ref[hidden:] = du
    delta_ref[:, :hidden] = dh.T
    delta_ref[:, hidden:] = du.T
    prob_ref[...] = jnp.sum(act_ref[...].astype(F32) * back, axis=0, keepdims=True)


def row_grad_kernel(pos_ref, delta_t_ref, prob_ref, wg_ref, wu_ref, *outs):
    width, hidden = wg_ref.shape[1:]
    size = 512
    for start in range(0, width, size):
        at = slice(start, start + size)
        rows_t = dot(wg_ref[0, at], delta_t_ref[:hidden]) + dot(wu_ref[0, at], delta_t_ref[hidden:])
        rows = rows_t.astype(BF16).T
        for j, out_ref in enumerate(outs):
            out_ref[:, at] = rows[j * CAP : (j + 1) * CAP]
    full = prob_ref[...]
    high = full.astype(BF16).astype(F32)
    lane = lax.broadcasted_iota(jnp.int32, (EXTRA, full.shape[1]), 0)
    both = jnp.where(lane == 0, high, jnp.where(lane == 1, full - high, 0.0)).T.astype(BF16)
    for j, out_ref in enumerate(outs):
        out_ref[:, width:] = both[j * CAP : (j + 1) * CAP]


def total_of(refs):
    down, *rest = [ref[0].astype(F32) for ref in refs]
    first = [down, rest[0] + rest[1], rest[2] + rest[3]]
    return sum(rest[4:], jnp.concatenate(first, axis=0))


def add_kernel(pos_ref, *rest):
    ins, outs = rest[:-2], rest[-2:]
    middle = len(ins) // 2
    for refs, out_ref in zip((ins[:middle], ins[middle:]), outs):
        out_ref[0] = total_of(refs).astype(BF16)


def add_pairs_kernel(pos_ref, a_ref, b_ref, c_ref, d_ref, low_ref, high_ref):
    low_ref[...] = (a_ref[...].astype(F32) + b_ref[...].astype(F32)).astype(BF16)
    high_ref[...] = (c_ref[...].astype(F32) + d_ref[...].astype(F32)).astype(BF16)


def add_all_kernel(pos_ref, *rest):
    ins, outs = rest[:-2], rest[-2:]
    middle = len(ins) // 2
    for refs, out_ref in zip((ins[:middle], ins[middle:]), outs):
        out_ref[...] = sum(ref[...].astype(F32) for ref in refs).astype(BF16)


def finish_first_kernel(pos_ref, *rest):
    ins, out_ref = rest[:-1], rest[-1]
    middle, half = len(ins) // 2, out_ref.shape[0] // 2
    out_ref[:half] = sum(ref[0].astype(F32) for ref in ins[:middle])
    out_ref[half:] = sum(ref[0].astype(F32) for ref in ins[middle:])


def combine_kernel(scale, pos_ref, place_ref, routes_ref, probs_ref, *rest):
    experts = (len(rest) - 2) // 2
    x_ref, prob_ref = rest[2 * experts :]
    rows = joined(rest[:experts])
    x_ref[...] = dot(place_ref[...], rows).astype(BF16)

    @pl.when(pl.program_id(0) == 0)
    def _():
        extra = joined(rest[experts : 2 * experts])
        tok, slots = place_ref.shape
        top = routes_ref.shape[0]
        place, expert = slot_matrix(routes_ref, pos_ref[1], slots)
        value = jnp.sum(extra.astype(F32), axis=1, keepdims=True)
        probs = probs_ref[...].astype(F32)
        line = lax.broadcasted_iota(jnp.int32, probs.shape, 0)
        result = jnp.zeros(probs.shape, F32)
        for k in range(top):
            mine = jnp.where(routes_ref[k : k + 1, :] == expert, place, 0.0)
            found = jnp.sum(mine * value, axis=0, keepdims=True)
            result += jnp.where(line == k, found, 0.0)
        prob_ref[...] = (result * scale / probs).astype(BF16)


def finish_kernel(
    pos_ref, first_ref, low_ref, low_last_ref, high_ref, high_last_ref, down_ref, gate_ref, up_ref
):
    rows = gate_ref.shape[0]
    down_rows = low_ref.shape[1] - 2 * rows
    early = down_ref.shape[1] - FIRST

    def total(ref, last_ref, start, stop):
        return ref[0, start:stop].astype(F32) + last_ref[0, start:stop].astype(F32)

    def write(ref, last_ref):
        gate_ref[...] = total(ref, last_ref, down_rows, down_rows + rows)
        up_ref[...] = total(ref, last_ref, down_rows + rows, down_rows + 2 * rows)

    @pl.when(pl.program_id(0) == 0)
    def _():
        down_ref[:, :FIRST] = first_ref[...].T
        if early:
            down_ref[:, FIRST:] = total(low_ref, low_last_ref, 0, early).T
        write(low_ref, low_last_ref)

    @pl.when(pl.program_id(0) == 1)
    def _():
        down_ref[:, : down_rows - early] = total(low_ref, low_last_ref, early, down_rows).T
        down_ref[:, down_rows - early :] = total(high_ref, high_last_ref, 0, down_rows).T
        write(high_ref, high_last_ref)


def flip(x, axis, bit):
    count = lax.axis_size(axis)
    return lax.ppermute(x, axis, [(i, i ^ bit) for i in range(count)])


def body(tokens, out_grad, routes, gate_probs, w_gate, w_up, w_down):
    tok, width = tokens.shape
    experts = lax.axis_size("expert")
    replicas = lax.axis_size("dp")
    hidden = w_gate.shape[2]
    slots = experts * CAP
    shard = width // replicas
    pieces = replicas // 2
    levels = pieces.bit_length() - 1
    grad_scale = 1.0 / math.sqrt(tok * replicas * experts)
    prob_scale = 1.0 / math.sqrt(width)
    pos = jnp.stack([lax.axis_index("dp"), lax.axis_index("expert")]).astype(jnp.int32)
    chain = []

    def run(kernel, grid, in_specs, out_specs, out_shape, args, after=(), **kw):
        out = call(
            kernel, grid, in_specs, out_specs, out_shape, pos, args, [*chain[-1:], *after], **kw
        )
        chain.append(out[-1])
        return out[:-1]

    def exchange(blocks):
        return [blocks[0]] + [flip(blocks[j], "expert", experts - j) for j in range(1, experts)]

    def block_specs(cols, at):
        return [pl.BlockSpec((CAP, cols), at) for _ in range(experts)]

    def cross(low, high, level):
        return flip(low, "dp", 2 << level), flip(high, "dp", 2 << (levels - 1 - level))

    half = shard // 2
    merged = (shard - FIRST) // 2 + 2 * half

    def add(halves, level, count, places):
        specs, arrays = [], []
        for high, (down, keep, came, *later) in enumerate(halves):

            def spec(size, first, behind, high=high):
                shift = 0 if high else behind
                return pl.BlockSpec(
                    (1, size, hidden),
                    lambda i, pos: (places[high](i) << shift, first, 0),
                )

            specs += [spec(down.shape[1], 0, level - 1)]
            specs += [spec(half, at, level - 1) for at in (0, 0, 1, 1)]
            arrays += [down, keep, came, keep, came]
            for at, array in enumerate(later):
                specs.append(spec(array.shape[1], 0, level - 2 - at))
                arrays.append(array)
        return run(
            add_kernel,
            (count,),
            specs,
            [pl.BlockSpec((1, merged, hidden), lambda i, pos: (i, 0, 0))] * 2,
            [shape_of((count, merged, hidden))] * 2,
            arrays,
        )

    def add_first(low_state, high_state, level):
        count = pieces >> (level + 1)
        places = lambda i: 2 * i + 1, lambda i: count + i
        specs = []
        for high, state in enumerate((low_state, high_state)):
            for at, array in enumerate(state):
                shift = 0 if high else level - 1 - max(at - 1, 0)
                specs.append(
                    pl.BlockSpec(
                        (1, *array.shape[1:]),
                        lambda i, pos, high=high, shift=shift: (places[high](i) << shift, 0, 0),
                    )
                )
        block = (1, FIRST // 2, hidden)
        return run(
            add_all_kernel,
            (count,),
            specs,
            [pl.BlockSpec(block, lambda i, pos: (i, 0, 0))] * 2,
            [shape_of((count, *block[1:]))] * 2,
            low_state + high_state,
        )

    def mark(after, cost):
        run(lambda pos_ref: None, (1,), [], [], [], [], after, cost=cost)

    blocks = [whole((CAP, width)) for _ in range(experts)]
    routes, gate_probs = routes.T, gate_probs.T
    x_out = run(
        functools.partial(send_tokens_kernel, shard),
        (1,),
        [whole(routes.shape), whole(tokens.shape)],
        [IN_VMEM] * experts,
        [shape_of((CAP, width))] * experts,
        [routes, tokens],
    )
    x_in = exchange(x_out)

    mark([], LONG)

    def send_cot(start, size, after):
        cols = size * replicas
        placed = start == 0
        out = run(
            functools.partial(send_cot_kernel, experts, shard, start),
            (1,),
            [whole(routes.shape), whole(gate_probs.shape), whole(out_grad.shape)],
            [IN_VMEM] * (experts + placed),
            [shape_of((CAP, cols))] * experts + [shape_of((tok, slots))] * placed,
            [routes, gate_probs, out_grad],
            after,
        )
        return exchange(out[:experts]), out[experts:]

    second = shard - FIRST
    dy_first, (place,) = send_cot(0, FIRST, [x_in[2]])
    dy, _ = send_cot(FIRST, second, [])

    def grad_near(rows_t, right, others):
        size = rows_t.shape[0] // replicas // 2 * (right.shape[1] // hidden)
        return run(
            functools.partial(grad_near_kernel, grad_scale, replicas),
            (1,),
            [IN_VMEM] * (2 + len(others)),
            [IN_VMEM] * 4,
            [shape_of((pieces // 2, size, hidden))] * 4,
            [rows_t, right, *others],
        )

    def grad_far(rows_t, right, count):
        out = run(
            functools.partial(grad_far_kernel, grad_scale, replicas),
            (1,),
            [IN_VMEM] * 2,
            [IN_VMEM] * count,
            [shape_of((rows_t.shape[0] // 2, right.shape[1] // count))] * count,
            [rows_t, right],
        )
        return [flip(part, "dp", 1) for part in out]

    def transpose(rows):
        (out,) = run(
            transpose_kernel,
            (1,),
            [IN_VMEM] * experts,
            [IN_VMEM],
            [shape_of((rows[0].shape[1], slots))],
            rows,
        )
        return out

    act, act_t, for_gate, for_up = run(
        functools.partial(forward_kernel, experts, 3),
        (1,),
        [IN_VMEM] * (experts + 2),
        [IN_VMEM] * 4,
        [shape_of((slots, hidden))] + [shape_of((hidden, slots), t) for t in (BF16, F32, F32)],
        [*x_in, w_gate, w_up],
        scratch=[pltpu.VMEM((slots, width), BF16)],
    )

    dy_t = transpose(dy_first)
    others = grad_far(dy_t, act, 1)
    (prev,) = run(
        functools.partial(back_first_kernel, shard),
        (1,),
        [IN_VMEM] * 2,
        [IN_VMEM],
        [shape_of((hidden, slots), F32)],
        [w_down, dy_t],
    )
    low_send, low_keep, high_send, high_keep = grad_near(dy_t, act, others)
    low, high = cross(low_send, high_send, 0)
    x_t = transpose(x_in)
    low_state, high_state = [low_keep, low], [high_keep, high]
    for level in range(1, levels):
        low, high = cross(*add_first(low_state, high_state, level), level)
        low_state.append(low)
        high_state.append(high)
    (down_first,) = run(
        finish_first_kernel,
        (1,),
        [whole((1, *a.shape[1:])) for a in low_state + high_state],
        [whole((FIRST, hidden))],
        [shape_of((FIRST, hidden), F32)],
        low_state + high_state,
    )

    dy_t = transpose(dy)
    others = grad_far(dy_t, act, 1)
    delta, delta_t, prob = run(
        functools.partial(back_hidden_kernel, shard),
        (1,),
        [IN_VMEM] * 6,
        [IN_VMEM] * 3,
        [
            shape_of((slots, 2 * hidden)),
            shape_of((2 * hidden, slots)),
            shape_of((1, slots), F32),
        ],
        [prev, w_down, dy_t, act_t, for_gate, for_up],
    )
    others_both = grad_far(x_t, delta, 3)
    low_send, low_keep, high_send, high_keep = grad_near(dy_t, act, others)
    down_low, down_high = cross(low_send, high_send, 0)
    down_keep = low_keep, high_keep

    back_out = run(
        row_grad_kernel,
        (1,),
        [IN_VMEM] * 4,
        [IN_VMEM] * experts,
        [shape_of((CAP, width + EXTRA))] * experts,
        [delta_t, prob, w_gate, w_up],
    )
    back_in = exchange(back_out)

    low_send, low_keep, high_send, high_keep = grad_near(x_t, delta, others_both)
    low, high = cross(low_send, high_send, 0)
    down_low, down_high = run(
        add_pairs_kernel,
        (1,),
        [whole(down_keep[0].shape)] * 4,
        [whole(down_keep[0].shape)] * 2,
        [shape_of(down_keep[0].shape)] * 2,
        [down_keep[0], down_low, down_keep[1], down_high],
    )
    mark([], LONG)
    halves = [[down_low, low_keep, low], [down_high, high_keep, high]]
    for level in range(1, levels):
        count = pieces >> (level + 1)
        places = lambda i: 2 * i + 1, lambda i, count=count: count + i
        low, high = cross(*add(halves, level, count, places), level)
        if level + 1 < levels:
            halves[0].append(low)
            halves[1].append(high)
    mine = add(halves, levels, 1, (lambda i: i, lambda i: i))

    step = width // 2
    x_grad, prob_grad = run(
        functools.partial(combine_kernel, prob_scale),
        (2,),
        [whole((tok, slots)), whole(routes.shape), whole(gate_probs.shape)]
        + block_specs(step, lambda i, pos: (0, i))
        + block_specs(EXTRA, lambda i, pos: (0, width // EXTRA)),
        [pl.BlockSpec((tok, step), lambda i, pos: (0, i)), whole(gate_probs.shape)],
        [shape_of((tok, width)), shape_of(gate_probs.shape)],
        [place, routes, gate_probs, *back_in, *back_in],
        cost=LONG,
    )
    down_grad, gate_grad, up_grad = run(
        finish_kernel,
        (2,),
        [whole(down_first.shape)] + [whole((1, merged, hidden))] * 4,
        [pl.BlockSpec((hidden, half), lambda i, pos: (0, i))]
        + [pl.BlockSpec((half, hidden), lambda i, pos: (i, 0))] * 2,
        [shape_of((hidden, shard), F32)] + [shape_of((shard, hidden), F32)] * 2,
        [down_first, mine[0], low, mine[1], high],
    )
    return (x_grad, prob_grad.T, gate_grad[None], up_grad[None], down_grad[None])


def solution(mesh):
    return jax.shard_map(
        body,
        mesh=mesh,
        in_specs=(
            P(("dp", "expert"), None),
            P(("dp", "expert"), None),
            P(("dp", "expert"), None),
            P(("dp", "expert"), None),
            P("expert", None, None),
            P("expert", None, None),
            P("expert", None, None),
        ),
        out_specs=(
            P(("dp", "expert"), None),
            P(("dp", "expert"), None),
            P("expert", "dp", None),
            P("expert", "dp", None),
            P("expert", None, "dp"),
        ),
        check_vma=False,
    )
```

```python
import functools
import math

import jax
import jax.numpy as jnp
from jax import lax
from jax.experimental import pallas as pl
from jax.experimental.pallas import tpu as pltpu
from jax.sharding import PartitionSpec as P

CAP = 64
FIRST = 128
EXTRA = 128
F32 = jnp.float32
BF16 = jnp.bfloat16
LONG = 6 * 10**10
VMEM_SPARE = 4 * 1024 * 1024


IN_VMEM = pl.BlockSpec(memory_space=pltpu.VMEM)


def whole(shape):
    return pl.BlockSpec(shape, lambda i, pos: (0,) * len(shape))


def call(kernel, grid, in_specs, out_specs, out_shape, pos, args, after, scratch=(), cost=1):
    held = sum(math.prod(ref.shape) * ref.dtype.itemsize for ref in scratch)
    for spec, array in zip([*in_specs, *out_specs], [*args, *out_shape]):
        if spec.block_shape is not None:
            held += 2 * math.prod(spec.block_shape) * array.dtype.itemsize
    first, count, last = 1 + len(args), len(after), len(out_shape)

    def ordered(*refs):
        outs = refs[first + count :]
        kernel(*refs[:first], *outs[:last], *outs[last + 1 :])
        outs[last][...] = jnp.zeros(outs[last].shape, F32)

    return pl.pallas_call(
        ordered,
        grid_spec=pltpu.PrefetchScalarGridSpec(
            num_scalar_prefetch=1,
            grid=grid,
            in_specs=list(in_specs) + [pl.BlockSpec(memory_space=pl.ANY)] * count,
            out_specs=[*out_specs, whole((8, 128))],
            scratch_shapes=list(scratch),
        ),
        out_shape=[*out_shape, shape_of((8, 128), F32)],
        compiler_params=pltpu.CompilerParams(vmem_limit_bytes=held + VMEM_SPARE),
        cost_estimate=pl.CostEstimate(flops=cost, bytes_accessed=1, transcendentals=0),
    )(pos, *args, *after)


def shape_of(shape, dtype=BF16):
    return jax.ShapeDtypeStruct(shape, dtype)


def dot(left, right):
    return jnp.dot(left, right, preferred_element_type=F32)


def shard_rows(relative, pos_ref, size):
    return pl.ds(pl.multiple_of((pos_ref[0] ^ relative) * size, size), size)


def slot_matrix(routes_ref, my_expert, slots):
    top, tok = routes_ref.shape
    index = lax.broadcasted_iota(jnp.int32, (slots, tok), 0)
    block = index // CAP
    expert = jnp.where(block == 0, 0, slots // CAP - block) ^ my_expert
    hit = jnp.zeros((slots, tok), jnp.bool_)
    for k in range(top):
        hit = hit | (routes_ref[k : k + 1, :] == expert)
    named = jnp.where(hit, 1.0, 0.0)
    before = lax.broadcasted_iota(jnp.int32, (tok, tok), 0) < lax.broadcasted_iota(
        jnp.int32, (tok, tok), 1
    )
    rank = dot(named.astype(BF16), jnp.where(before, 1.0, 0.0).astype(BF16))
    return jnp.where(rank == (index % CAP).astype(F32), named, 0.0), expert


def send_rows(place, ref, start, shard, outs):
    size = outs[0].shape[1] * shard // ref.shape[1]
    for i in range(ref.shape[1] // shard):
        rows = dot(place, ref[:, i * shard + start : i * shard + start + size]).astype(BF16)
        for j, out_ref in enumerate(outs):
            out_ref[:, i * size : (i + 1) * size] = rows[j * CAP : (j + 1) * CAP]


def send_tokens_kernel(shard, pos_ref, routes_ref, tok_ref, *outs):
    place, _ = slot_matrix(routes_ref, pos_ref[1], len(outs) * CAP)
    send_rows(place.astype(BF16), tok_ref, 0, shard, outs)


def send_cot_kernel(experts, shard, start, pos_ref, routes_ref, probs_ref, cot_ref, *rest):
    outs, place_t_ref = rest[:experts], rest[experts:]
    place, expert = slot_matrix(routes_ref, pos_ref[1], experts * CAP)
    probs = probs_ref[...].astype(F32)
    weight = jnp.zeros_like(place)
    for k in range(routes_ref.shape[0]):
        weight += jnp.where(routes_ref[k : k + 1, :] == expert, probs[k : k + 1, :], 0.0)
    send_rows((place * weight).astype(BF16), cot_ref, start, shard, outs)
    if place_t_ref:
        place_t_ref[0][...] = place.T.astype(BF16)


def joined(refs):
    return jnp.concatenate([ref[...] for ref in refs], axis=0)


def forward_kernel(experts, blocks, pos_ref, *rest):
    xs, (wg_ref, wu_ref), outs, x_ref = (
        rest[:experts],
        rest[experts : experts + 2],
        rest[experts + 2 : -1],
        rest[-1],
    )
    act_ref, act_t_ref, for_gate_ref, for_up_ref = outs
    for j in range(experts):
        x_ref[j * CAP : (j + 1) * CAP, :] = xs[j][...]
    size = wg_ref.shape[2] // blocks
    for i in range(blocks):
        at = slice(i * size, (i + 1) * size)
        gate = dot(x_ref[...], wg_ref[0, :, at]).T
        up = dot(x_ref[...], wu_ref[0, :, at]).T
        sig = jax.nn.sigmoid(gate)
        silu = gate * sig
        act = (silu * up).astype(BF16)
        act_ref[:, at] = act.T
        act_t_ref[at] = act
        for_gate_ref[at] = up * sig * (1.0 + gate * (1.0 - sig))
        for_up_ref[at] = silu


def transpose_kernel(pos_ref, *rest):
    ins, out_ref = rest[:-1], rest[-1]
    size = 512
    for at in range(0, out_ref.shape[0], size):
        rows = [ref[:, at : at + size] for ref in ins]
        out_ref[at : at + size] = jnp.concatenate(rows, axis=0).T


def transpose_far_kernel(scale, replicas, pos_ref, right_ref, *rest):
    ins, (out_ref, far_ref) = rest[:-2], rest[-2:]
    transpose_kernel(pos_ref, *ins, out_ref)
    grad_far_kernel(scale, replicas, pos_ref, out_ref, right_ref, far_ref)


def grad_far_kernel(scale, replicas, pos_ref, rows_ref, right_ref, *outs):
    size = rows_ref.shape[0] // replicas
    cols = outs[0].shape[1]
    for i in range(replicas // 2):
        rows = rows_ref[shard_rows(2 * i + 1, pos_ref, size), :]
        part = (dot(rows, right_ref[...]) * scale).astype(BF16)
        for at, out_ref in enumerate(outs):
            out_ref[i * size : (i + 1) * size] = part[:, at * cols : (at + 1) * cols]


def grad_near_kernel(scale, replicas, pos_ref, rows_ref, right_ref, *rest):
    others, (low_send, low_keep, high_send, high_keep) = rest[:-4], rest[-4:]
    size = rows_ref.shape[0] // replicas
    cols = low_keep.shape[2]
    half, count = size // 2, replicas // 4
    for q in range(replicas // 2):
        rows = rows_ref[shard_rows(2 * q, pos_ref, size), :]
        low_ref = low_send if q % 2 else low_keep
        high_ref, place = (high_send, q - count) if q >= count else (high_keep, q)
        came = [ref[q * size : (q + 1) * size] for ref in others]
        came = jnp.concatenate(came, axis=1).astype(F32)
        total = (dot(rows, right_ref[...]) * scale + came).astype(BF16)
        for at in range(total.shape[1] // cols):
            part = total[:, at * cols : (at + 1) * cols]
            low_ref[q // 2, at * half : (at + 1) * half] = part[:half]
            high_ref[place, at * half : (at + 1) * half] = part[half:]


def back_sum(wd_ref, rows_ref, start, shard):
    count = wd_ref.shape[2] // shard
    size = rows_ref.shape[0] // count
    return sum(
        dot(
            wd_ref[0, :, i * shard + start : i * shard + start + size],
            rows_ref[i * size : (i + 1) * size],
        )
        for i in range(count)
    )


def back_first_kernel(shard, pos_ref, wd_ref, rows_ref, out_ref):
    out_ref[...] = back_sum(wd_ref, rows_ref, 0, shard)


def back_hidden_kernel(
    shard,
    pos_ref,
    prev_ref,
    wd_ref,
    rows_ref,
    act_ref,
    for_gate_ref,
    for_up_ref,
    delta_ref,
    delta_t_ref,
    prob_ref,
):
    back = prev_ref[...] + back_sum(wd_ref, rows_ref, FIRST, shard)
    dh = (back * for_gate_ref[...]).astype(BF16)
    du = (back * for_up_ref[...]).astype(BF16)
    hidden = back.shape[0]
    delta_t_ref[:hidden] = dh
    delta_t_ref[hidden:] = du
    delta_ref[:, :hidden] = dh.T
    delta_ref[:, hidden:] = du.T
    prob_ref[...] = jnp.sum(act_ref[...].astype(F32) * back, axis=0, keepdims=True)


def row_grad_kernel(pos_ref, delta_t_ref, prob_ref, wg_ref, wu_ref, *outs):
    width, hidden = wg_ref.shape[1:]
    size = 512
    for start in range(0, width, size):
        at = slice(start, start + size)
        rows_t = dot(wg_ref[0, at], delta_t_ref[:hidden]) + dot(wu_ref[0, at], delta_t_ref[hidden:])
        rows = rows_t.astype(BF16).T
        for j, out_ref in enumerate(outs):
            out_ref[:, at] = rows[j * CAP : (j + 1) * CAP]
    full = prob_ref[...]
    high = full.astype(BF16).astype(F32)
    lane = lax.broadcasted_iota(jnp.int32, (EXTRA, full.shape[1]), 0)
    both = jnp.where(lane == 0, high, jnp.where(lane == 1, full - high, 0.0)).T.astype(BF16)
    for j, out_ref in enumerate(outs):
        out_ref[:, width:] = both[j * CAP : (j + 1) * CAP]


def total_of(refs):
    down, *rest = [ref[0].astype(F32) for ref in refs]
    first = [down, rest[0] + rest[1], rest[2] + rest[3]]
    return sum(rest[4:], jnp.concatenate(first, axis=0))


def add_kernel(pos_ref, *rest):
    ins, outs = rest[:-2], rest[-2:]
    middle = len(ins) // 2
    for refs, out_ref in zip((ins[:middle], ins[middle:]), outs):
        out_ref[0] = total_of(refs).astype(BF16)


def add_pairs_kernel(pos_ref, a_ref, b_ref, c_ref, d_ref, low_ref, high_ref):
    low_ref[...] = (a_ref[...].astype(F32) + b_ref[...].astype(F32)).astype(BF16)
    high_ref[...] = (c_ref[...].astype(F32) + d_ref[...].astype(F32)).astype(BF16)


def add_all_kernel(pos_ref, *rest):
    ins, outs = rest[:-2], rest[-2:]
    middle = len(ins) // 2
    for refs, out_ref in zip((ins[:middle], ins[middle:]), outs):
        out_ref[...] = sum(ref[...].astype(F32) for ref in refs).astype(BF16)


def finish_first_kernel(pos_ref, *rest):
    ins, out_ref = rest[:-1], rest[-1]
    middle, half = len(ins) // 2, out_ref.shape[0] // 2
    out_ref[:half] = sum(ref[0].astype(F32) for ref in ins[:middle])
    out_ref[half:] = sum(ref[0].astype(F32) for ref in ins[middle:])


def combine_kernel(scale, pos_ref, place_ref, routes_ref, probs_ref, *rest):
    experts = (len(rest) - 2) // 2
    x_ref, prob_ref = rest[2 * experts :]
    rows = joined(rest[:experts])
    x_ref[...] = dot(place_ref[...], rows).astype(BF16)

    @pl.when(pl.program_id(0) == 0)
    def _():
        extra = joined(rest[experts : 2 * experts])
        tok, slots = place_ref.shape
        top = routes_ref.shape[0]
        place, expert = slot_matrix(routes_ref, pos_ref[1], slots)
        value = jnp.sum(extra.astype(F32), axis=1, keepdims=True)
        probs = probs_ref[...].astype(F32)
        line = lax.broadcasted_iota(jnp.int32, probs.shape, 0)
        result = jnp.zeros(probs.shape, F32)
        for k in range(top):
            mine = jnp.where(routes_ref[k : k + 1, :] == expert, place, 0.0)
            found = jnp.sum(mine * value, axis=0, keepdims=True)
            result += jnp.where(line == k, found, 0.0)
        prob_ref[...] = (result * scale / probs).astype(BF16)


def finish_kernel(
    pos_ref, first_ref, low_ref, low_last_ref, high_ref, high_last_ref, down_ref, gate_ref, up_ref
):
    rows = gate_ref.shape[0]
    down_rows = low_ref.shape[1] - 2 * rows
    early = down_ref.shape[1] - FIRST

    def total(ref, last_ref, start, stop):
        return ref[0, start:stop].astype(F32) + last_ref[0, start:stop].astype(F32)

    def write(ref, last_ref):
        gate_ref[...] = total(ref, last_ref, down_rows, down_rows + rows)
        up_ref[...] = total(ref, last_ref, down_rows + rows, down_rows + 2 * rows)

    @pl.when(pl.program_id(0) == 0)
    def _():
        down_ref[:, :FIRST] = first_ref[...].T
        if early:
            down_ref[:, FIRST:] = total(low_ref, low_last_ref, 0, early).T
        write(low_ref, low_last_ref)

    @pl.when(pl.program_id(0) == 1)
    def _():
        down_ref[:, : down_rows - early] = total(low_ref, low_last_ref, early, down_rows).T
        down_ref[:, down_rows - early :] = total(high_ref, high_last_ref, 0, down_rows).T
        write(high_ref, high_last_ref)


def flip(x, axis, bit):
    count = lax.axis_size(axis)
    return lax.ppermute(x, axis, [(i, i ^ bit) for i in range(count)])


def body(tokens, out_grad, routes, gate_probs, w_gate, w_up, w_down):
    tok, width = tokens.shape
    experts = lax.axis_size("expert")
    replicas = lax.axis_size("dp")
    hidden = w_gate.shape[2]
    slots = experts * CAP
    shard = width // replicas
    pieces = replicas // 2
    levels = pieces.bit_length() - 1
    grad_scale = 1.0 / math.sqrt(tok * replicas * experts)
    prob_scale = 1.0 / math.sqrt(width)
    pos = jnp.stack([lax.axis_index("dp"), lax.axis_index("expert")]).astype(jnp.int32)
    chain = []

    def run(kernel, grid, in_specs, out_specs, out_shape, args, after=(), **kw):
        out = call(
            kernel, grid, in_specs, out_specs, out_shape, pos, args, [*chain[-1:], *after], **kw
        )
        chain.append(out[-1])
        return out[:-1]

    def exchange(blocks):
        return [blocks[0]] + [flip(blocks[j], "expert", experts - j) for j in range(1, experts)]

    def block_specs(cols, at):
        return [pl.BlockSpec((CAP, cols), at) for _ in range(experts)]

    def cross(low, high, level):
        return flip(low, "dp", 2 << level), flip(high, "dp", 2 << (levels - 1 - level))

    half = shard // 2
    merged = (shard - FIRST) // 2 + 2 * half

    def add(halves, level, count, places):
        specs, arrays = [], []
        for high, (down, keep, came, *later) in enumerate(halves):

            def spec(size, first, behind, high=high):
                shift = 0 if high else behind
                return pl.BlockSpec(
                    (1, size, hidden),
                    lambda i, pos: (places[high](i) << shift, first, 0),
                )

            specs += [spec(down.shape[1], 0, level - 1)]
            specs += [spec(half, at, level - 1) for at in (0, 0, 1, 1)]
            arrays += [down, keep, came, keep, came]
            for at, array in enumerate(later):
                specs.append(spec(array.shape[1], 0, level - 2 - at))
                arrays.append(array)
        return run(
            add_kernel,
            (count,),
            specs,
            [pl.BlockSpec((1, merged, hidden), lambda i, pos: (i, 0, 0))] * 2,
            [shape_of((count, merged, hidden))] * 2,
            arrays,
        )

    def add_first(low_state, high_state, level):
        count = pieces >> (level + 1)
        places = lambda i: 2 * i + 1, lambda i: count + i
        specs = []
        for high, state in enumerate((low_state, high_state)):
            for at, array in enumerate(state):
                shift = 0 if high else level - 1 - max(at - 1, 0)
                specs.append(
                    pl.BlockSpec(
                        (1, *array.shape[1:]),
                        lambda i, pos, high=high, shift=shift: (places[high](i) << shift, 0, 0),
                    )
                )
        block = (1, FIRST // 2, hidden)
        return run(
            add_all_kernel,
            (count,),
            specs,
            [pl.BlockSpec(block, lambda i, pos: (i, 0, 0))] * 2,
            [shape_of((count, *block[1:]))] * 2,
            low_state + high_state,
        )

    def mark(after, cost):
        run(lambda pos_ref: None, (1,), [], [], [], [], after, cost=cost)

    blocks = [whole((CAP, width)) for _ in range(experts)]
    routes, gate_probs = routes.T, gate_probs.T
    x_out = run(
        functools.partial(send_tokens_kernel, shard),
        (1,),
        [whole(routes.shape), whole(tokens.shape)],
        [IN_VMEM] * experts,
        [shape_of((CAP, width))] * experts,
        [routes, tokens],
    )
    x_in = exchange(x_out)

    mark([], LONG)

    def send_cot(start, size, after):
        cols = size * replicas
        placed = start == 0
        out = run(
            functools.partial(send_cot_kernel, experts, shard, start),
            (1,),
            [whole(routes.shape), whole(gate_probs.shape), whole(out_grad.shape)],
            [IN_VMEM] * (experts + placed),
            [shape_of((CAP, cols))] * experts + [shape_of((tok, slots))] * placed,
            [routes, gate_probs, out_grad],
            after,
        )
        return exchange(out[:experts]), out[experts:]

    second = shard - FIRST
    dy_first, (place,) = send_cot(0, FIRST, [x_in[1]])
    dy, _ = send_cot(FIRST, second, [])

    def grad_near(rows_t, right, others):
        size = rows_t.shape[0] // replicas // 2 * (right.shape[1] // hidden)
        return run(
            functools.partial(grad_near_kernel, grad_scale, replicas),
            (1,),
            [IN_VMEM] * (2 + len(others)),
            [IN_VMEM] * 4,
            [shape_of((pieces // 2, size, hidden))] * 4,
            [rows_t, right, *others],
        )

    def transpose_far(rows):
        cols = rows[0].shape[1]
        rows_t, far = run(
            functools.partial(transpose_far_kernel, grad_scale, replicas),
            (1,),
            [IN_VMEM] * (1 + experts),
            [IN_VMEM] * 2,
            [shape_of((cols, slots)), shape_of((cols // 2, hidden))],
            [act, *rows],
        )
        return rows_t, flip(far, "dp", 1)

    def transpose(rows):
        (out,) = run(
            transpose_kernel,
            (1,),
            [IN_VMEM] * experts,
            [IN_VMEM],
            [shape_of((rows[0].shape[1], slots))],
            rows,
        )
        return out

    act, act_t, for_gate, for_up = run(
        functools.partial(forward_kernel, experts, 3),
        (1,),
        [IN_VMEM] * (experts + 2),
        [IN_VMEM] * 4,
        [shape_of((slots, hidden))] + [shape_of((hidden, slots), t) for t in (BF16, F32, F32)],
        [*x_in, w_gate, w_up],
        scratch=[pltpu.VMEM((slots, width), BF16)],
    )

    dy_t, other = transpose_far(dy_first)
    (prev,) = run(
        functools.partial(back_first_kernel, shard),
        (1,),
        [IN_VMEM] * 2,
        [IN_VMEM],
        [shape_of((hidden, slots), F32)],
        [w_down, dy_t],
    )
    low_send, low_keep, high_send, high_keep = grad_near(dy_t, act, [other])
    low, high = cross(low_send, high_send, 0)
    x_t = transpose(x_in)
    low_state, high_state = [low_keep, low], [high_keep, high]
    for level in range(1, levels):
        low, high = cross(*add_first(low_state, high_state, level), level)
        low_state.append(low)
        high_state.append(high)
    (down_first,) = run(
        finish_first_kernel,
        (1,),
        [whole((1, *a.shape[1:])) for a in low_state + high_state],
        [whole((FIRST, hidden))],
        [shape_of((FIRST, hidden), F32)],
        low_state + high_state,
    )

    dy_t, other = transpose_far(dy)
    delta, delta_t, prob = run(
        functools.partial(back_hidden_kernel, shard),
        (1,),
        [IN_VMEM] * 6,
        [IN_VMEM] * 3,
        [
            shape_of((slots, 2 * hidden)),
            shape_of((2 * hidden, slots)),
            shape_of((1, slots), F32),
        ],
        [prev, w_down, dy_t, act_t, for_gate, for_up],
    )
    far = run(
        functools.partial(grad_far_kernel, grad_scale, replicas),
        (1,),
        [IN_VMEM] * 2,
        [IN_VMEM] * 3,
        [shape_of((width // 2, 2 * hidden // 3))] * 3,
        [x_t, delta],
    )
    others = [flip(part, "dp", 1) for part in far]
    low_send, low_keep, high_send, high_keep = grad_near(dy_t, act, [other])
    down_low, down_high = cross(low_send, high_send, 0)
    down_keep = low_keep, high_keep

    back_out = run(
        row_grad_kernel,
        (1,),
        [IN_VMEM] * 4,
        [IN_VMEM] * experts,
        [shape_of((CAP, width + EXTRA))] * experts,
        [delta_t, prob, w_gate, w_up],
    )
    back_in = exchange(back_out)

    low_send, low_keep, high_send, high_keep = grad_near(x_t, delta, others)
    low, high = cross(low_send, high_send, 0)
    down_low, down_high = run(
        add_pairs_kernel,
        (1,),
        [whole(down_keep[0].shape)] * 4,
        [whole(down_keep[0].shape)] * 2,
        [shape_of(down_keep[0].shape)] * 2,
        [down_keep[0], down_low, down_keep[1], down_high],
    )
    mark([], LONG)
    halves = [[down_low, low_keep, low], [down_high, high_keep, high]]
    for level in range(1, levels):
        count = pieces >> (level + 1)
        places = lambda i: 2 * i + 1, lambda i, count=count: count + i
        low, high = cross(*add(halves, level, count, places), level)
        if level + 1 < levels:
            halves[0].append(low)
            halves[1].append(high)
    mine = add(halves, levels, 1, (lambda i: i, lambda i: i))

    step = width // 2
    x_grad, prob_grad = run(
        functools.partial(combine_kernel, prob_scale),
        (2,),
        [whole((tok, slots)), whole(routes.shape), whole(gate_probs.shape)]
        + block_specs(step, lambda i, pos: (0, i))
        + block_specs(EXTRA, lambda i, pos: (0, width // EXTRA)),
        [pl.BlockSpec((tok, step), lambda i, pos: (0, i)), whole(gate_probs.shape)],
        [shape_of((tok, width)), shape_of(gate_probs.shape)],
        [place, routes, gate_probs, *back_in, *back_in],
        cost=LONG,
    )
    down_grad, gate_grad, up_grad = run(
        finish_kernel,
        (2,),
        [whole(down_first.shape)] + [whole((1, merged, hidden))] * 4,
        [pl.BlockSpec((hidden, half), lambda i, pos: (0, i))]
        + [pl.BlockSpec((half, hidden), lambda i, pos: (i, 0))] * 2,
        [shape_of((hidden, shard), F32)] + [shape_of((shard, hidden), F32)] * 2,
        [down_first, mine[0], low, mine[1], high],
    )
    return (x_grad, prob_grad.T, gate_grad[None], up_grad[None], down_grad[None])


def solution(mesh):
    return jax.shard_map(
        body,
        mesh=mesh,
        in_specs=(
            P(("dp", "expert"), None),
            P(("dp", "expert"), None),
            P(("dp", "expert"), None),
            P(("dp", "expert"), None),
            P("expert", None, None),
            P("expert", None, None),
            P("expert", None, None),
        ),
        out_specs=(
            P(("dp", "expert"), None),
            P(("dp", "expert"), None),
            P("expert", "dp", None),
            P("expert", "dp", None),
            P("expert", None, "dp"),
        ),
        check_vma=False,
    )
```

```python
import functools
import math

import jax
import jax.numpy as jnp
from jax import lax
from jax.experimental import pallas as pl
from jax.experimental.pallas import tpu as pltpu
from jax.sharding import PartitionSpec as P

CAP = 64
FIRST = 128
EXTRA = 128
F32 = jnp.float32
BF16 = jnp.bfloat16
LONG = 6 * 10**10
VMEM_SPARE = 4 * 1024 * 1024


IN_VMEM = pl.BlockSpec(memory_space=pltpu.VMEM)


def whole(shape):
    return pl.BlockSpec(shape, lambda i, pos: (0,) * len(shape))


def call(kernel, grid, in_specs, out_specs, out_shape, pos, args, after, scratch=(), cost=1):
    held = sum(math.prod(ref.shape) * ref.dtype.itemsize for ref in scratch)
    for spec, array in zip([*in_specs, *out_specs], [*args, *out_shape]):
        if spec.block_shape is not None:
            held += 2 * math.prod(spec.block_shape) * array.dtype.itemsize
    first, count, last = 1 + len(args), len(after), len(out_shape)

    def ordered(*refs):
        outs = refs[first + count :]
        kernel(*refs[:first], *outs[:last], *outs[last + 1 :])
        outs[last][...] = jnp.zeros(outs[last].shape, F32)

    return pl.pallas_call(
        ordered,
        grid_spec=pltpu.PrefetchScalarGridSpec(
            num_scalar_prefetch=1,
            grid=grid,
            in_specs=list(in_specs) + [pl.BlockSpec(memory_space=pl.ANY)] * count,
            out_specs=[*out_specs, whole((8, 128))],
            scratch_shapes=list(scratch),
        ),
        out_shape=[*out_shape, shape_of((8, 128), F32)],
        compiler_params=pltpu.CompilerParams(vmem_limit_bytes=held + VMEM_SPARE),
        cost_estimate=pl.CostEstimate(flops=cost, bytes_accessed=1, transcendentals=0),
    )(pos, *args, *after)


def shape_of(shape, dtype=BF16):
    return jax.ShapeDtypeStruct(shape, dtype)


def dot(left, right):
    return jnp.dot(left, right, preferred_element_type=F32)


def shard_rows(relative, pos_ref, stride, start):
    at = (pos_ref[0] ^ relative) * stride + start
    return pl.ds(pl.multiple_of(at, math.gcd(stride, start)), stride - start)


def slot_matrix(routes_ref, my_expert, slots):
    top, tok = routes_ref.shape
    index = lax.broadcasted_iota(jnp.int32, (slots, tok), 0)
    block = index // CAP
    expert = jnp.where(block == 0, 0, slots // CAP - block) ^ my_expert
    hit = jnp.zeros((slots, tok), jnp.bool_)
    for k in range(top):
        hit = hit | (routes_ref[k : k + 1, :] == expert)
    named = jnp.where(hit, 1.0, 0.0)
    before = lax.broadcasted_iota(jnp.int32, (tok, tok), 0) < lax.broadcasted_iota(
        jnp.int32, (tok, tok), 1
    )
    rank = dot(named.astype(BF16), jnp.where(before, 1.0, 0.0).astype(BF16))
    return jnp.where(rank == (index % CAP).astype(F32), named, 0.0), expert


def send_rows(place, ref, start, shard, outs):
    size = outs[0].shape[1] * shard // ref.shape[1]
    for i in range(ref.shape[1] // shard):
        rows = dot(place, ref[:, i * shard + start : i * shard + start + size]).astype(BF16)
        for j, out_ref in enumerate(outs):
            out_ref[:, i * size : (i + 1) * size] = rows[j * CAP : (j + 1) * CAP]


def send_tokens_kernel(shard, pos_ref, routes_ref, tok_ref, *outs):
    place, _ = slot_matrix(routes_ref, pos_ref[1], len(outs) * CAP)
    send_rows(place.astype(BF16), tok_ref, 0, shard, outs)


def send_cot_kernel(experts, shard, start, pos_ref, routes_ref, probs_ref, cot_ref, *rest):
    outs, place_t_ref = rest[:experts], rest[experts:]
    place, expert = slot_matrix(routes_ref, pos_ref[1], experts * CAP)
    probs = probs_ref[...].astype(F32)
    weight = jnp.zeros_like(place)
    for k in range(routes_ref.shape[0]):
        weight += jnp.where(routes_ref[k : k + 1, :] == expert, probs[k : k + 1, :], 0.0)
    send_rows((place * weight).astype(BF16), cot_ref, start, shard, outs)
    if place_t_ref:
        place_t_ref[0][...] = place.T.astype(BF16)


def joined(refs):
    return jnp.concatenate([ref[...] for ref in refs], axis=0)


def forward_kernel(experts, blocks, pos_ref, *rest):
    xs, (wg_ref, wu_ref), outs, x_ref = (
        rest[:experts],
        rest[experts : experts + 2],
        rest[experts + 2 : -1],
        rest[-1],
    )
    act_ref, act_t_ref, for_gate_ref, for_up_ref = outs
    for j in range(experts):
        x_ref[j * CAP : (j + 1) * CAP, :] = xs[j][...]
    size = wg_ref.shape[2] // blocks
    for i in range(blocks):
        at = slice(i * size, (i + 1) * size)
        gate = dot(x_ref[...], wg_ref[0, :, at]).T
        up = dot(x_ref[...], wu_ref[0, :, at]).T
        sig = jax.nn.sigmoid(gate)
        silu = gate * sig
        act = (silu * up).astype(BF16)
        act_ref[:, at] = act.T
        act_t_ref[at] = act
        for_gate_ref[at] = up * sig * (1.0 + gate * (1.0 - sig))
        for_up_ref[at] = silu


def transpose_kernel(pos_ref, *rest):
    ins, out_ref = rest[:-1], rest[-1]
    size = 512
    for at in range(0, out_ref.shape[0], size):
        rows = [ref[:, at : at + size] for ref in ins]
        out_ref[at : at + size] = jnp.concatenate(rows, axis=0).T


def transpose_far_kernel(scale, replicas, pos_ref, right_ref, *rest):
    ins, (out_ref, far_ref) = rest[:-2], rest[-2:]
    transpose_kernel(pos_ref, *ins, out_ref)
    grad_far_kernel(scale, replicas, 0, pos_ref, out_ref, right_ref, far_ref)


def transpose_rest_kernel(scale, replicas, pos_ref, right_ref, first_ref, *rest):
    ins, (out_ref, far_ref) = rest[:-2], rest[-2:]
    stride = out_ref.shape[0] // replicas
    size = stride - FIRST
    for i in range(replicas):
        at = i * stride
        out_ref[at : at + FIRST] = first_ref[i * FIRST : (i + 1) * FIRST]
        rows = [ref[:, i * size : (i + 1) * size] for ref in ins]
        out_ref[at + FIRST : at + stride] = jnp.concatenate(rows, axis=0).T
    grad_far_kernel(scale, replicas, FIRST, pos_ref, out_ref, right_ref, far_ref)


def grad_far_kernel(scale, replicas, start, pos_ref, rows_ref, right_ref, *outs):
    stride = rows_ref.shape[0] // replicas
    size, cols = stride - start, outs[0].shape[1]
    for i in range(replicas // 2):
        rows = rows_ref[shard_rows(2 * i + 1, pos_ref, stride, start), :]
        part = (dot(rows, right_ref[...]) * scale).astype(BF16)
        for at, out_ref in enumerate(outs):
            out_ref[i * size : (i + 1) * size] = part[:, at * cols : (at + 1) * cols]


def grad_near_kernel(scale, replicas, start, pos_ref, rows_ref, right_ref, *rest):
    others, (low_send, low_keep, high_send, high_keep) = rest[:-4], rest[-4:]
    stride = rows_ref.shape[0] // replicas
    size, cols = stride - start, low_keep.shape[2]
    half, count = size // 2, replicas // 4
    for q in range(replicas // 2):
        rows = rows_ref[shard_rows(2 * q, pos_ref, stride, start), :]
        low_ref = low_send if q % 2 else low_keep
        high_ref, place = (high_send, q - count) if q >= count else (high_keep, q)
        came = [ref[q * size : (q + 1) * size] for ref in others]
        came = jnp.concatenate(came, axis=1).astype(F32)
        total = (dot(rows, right_ref[...]) * scale + came).astype(BF16)
        for at in range(total.shape[1] // cols):
            part = total[:, at * cols : (at + 1) * cols]
            low_ref[q // 2, at * half : (at + 1) * half] = part[:half]
            high_ref[place, at * half : (at + 1) * half] = part[half:]


def back_hidden_kernel(
    pos_ref,
    wd_ref,
    rows_ref,
    act_ref,
    for_gate_ref,
    for_up_ref,
    delta_ref,
    delta_t_ref,
    prob_ref,
):
    back = dot(wd_ref[0], rows_ref[...])
    dh = (back * for_gate_ref[...]).astype(BF16)
    du = (back * for_up_ref[...]).astype(BF16)
    hidden = back.shape[0]
    delta_t_ref[:hidden] = dh
    delta_t_ref[hidden:] = du
    delta_ref[:, :hidden] = dh.T
    delta_ref[:, hidden:] = du.T
    prob_ref[...] = jnp.sum(act_ref[...].astype(F32) * back, axis=0, keepdims=True)


def row_grad_kernel(pos_ref, delta_t_ref, prob_ref, wg_ref, wu_ref, *outs):
    width, hidden = wg_ref.shape[1:]
    size = 512
    for start in range(0, width, size):
        at = slice(start, start + size)
        rows_t = dot(wg_ref[0, at], delta_t_ref[:hidden]) + dot(wu_ref[0, at], delta_t_ref[hidden:])
        rows = rows_t.astype(BF16).T
        for j, out_ref in enumerate(outs):
            out_ref[:, at] = rows[j * CAP : (j + 1) * CAP]
    full = prob_ref[...]
    high = full.astype(BF16).astype(F32)
    lane = lax.broadcasted_iota(jnp.int32, (EXTRA, full.shape[1]), 0)
    both = jnp.where(lane == 0, high, jnp.where(lane == 1, full - high, 0.0)).T.astype(BF16)
    for j, out_ref in enumerate(outs):
        out_ref[:, width:] = both[j * CAP : (j + 1) * CAP]


def total_of(refs):
    down, *rest = [ref[0].astype(F32) for ref in refs]
    first = [down, rest[0] + rest[1], rest[2] + rest[3]]
    return sum(rest[4:], jnp.concatenate(first, axis=0))


def add_kernel(pos_ref, *rest):
    ins, outs = rest[:-2], rest[-2:]
    middle = len(ins) // 2
    for refs, out_ref in zip((ins[:middle], ins[middle:]), outs):
        out_ref[0] = total_of(refs).astype(BF16)


def add_pairs_kernel(pos_ref, a_ref, b_ref, c_ref, d_ref, low_ref, high_ref):
    low_ref[...] = (a_ref[...].astype(F32) + b_ref[...].astype(F32)).astype(BF16)
    high_ref[...] = (c_ref[...].astype(F32) + d_ref[...].astype(F32)).astype(BF16)


def add_all_kernel(pos_ref, *rest):
    ins, outs = rest[:-2], rest[-2:]
    middle = len(ins) // 2
    for refs, out_ref in zip((ins[:middle], ins[middle:]), outs):
        out_ref[...] = sum(ref[...].astype(F32) for ref in refs).astype(BF16)


def finish_first_kernel(pos_ref, *rest):
    ins, out_ref = rest[:-1], rest[-1]
    middle, half = len(ins) // 2, out_ref.shape[0] // 2
    out_ref[:half] = sum(ref[0].astype(F32) for ref in ins[:middle])
    out_ref[half:] = sum(ref[0].astype(F32) for ref in ins[middle:])


def combine_kernel(scale, pos_ref, place_ref, routes_ref, probs_ref, *rest):
    experts = (len(rest) - 2) // 2
    x_ref, prob_ref = rest[2 * experts :]
    rows = joined(rest[:experts])
    x_ref[...] = dot(place_ref[...], rows).astype(BF16)

    @pl.when(pl.program_id(0) == 0)
    def _():
        extra = joined(rest[experts : 2 * experts])
        tok, slots = place_ref.shape
        top = routes_ref.shape[0]
        place, expert = slot_matrix(routes_ref, pos_ref[1], slots)
        value = jnp.sum(extra.astype(F32), axis=1, keepdims=True)
        probs = probs_ref[...].astype(F32)
        line = lax.broadcasted_iota(jnp.int32, probs.shape, 0)
        result = jnp.zeros(probs.shape, F32)
        for k in range(top):
            mine = jnp.where(routes_ref[k : k + 1, :] == expert, place, 0.0)
            found = jnp.sum(mine * value, axis=0, keepdims=True)
            result += jnp.where(line == k, found, 0.0)
        prob_ref[...] = (result * scale / probs).astype(BF16)


def finish_kernel(
    pos_ref, first_ref, low_ref, low_last_ref, high_ref, high_last_ref, down_ref, gate_ref, up_ref
):
    rows = gate_ref.shape[0]
    down_rows = low_ref.shape[1] - 2 * rows
    early = down_ref.shape[1] - FIRST

    def total(ref, last_ref, start, stop):
        return ref[0, start:stop].astype(F32) + last_ref[0, start:stop].astype(F32)

    def write(ref, last_ref):
        gate_ref[...] = total(ref, last_ref, down_rows, down_rows + rows)
        up_ref[...] = total(ref, last_ref, down_rows + rows, down_rows + 2 * rows)

    @pl.when(pl.program_id(0) == 0)
    def _():
        down_ref[:, :FIRST] = first_ref[...].T
        if early:
            down_ref[:, FIRST:] = total(low_ref, low_last_ref, 0, early).T
        write(low_ref, low_last_ref)

    @pl.when(pl.program_id(0) == 1)
    def _():
        down_ref[:, : down_rows - early] = total(low_ref, low_last_ref, early, down_rows).T
        down_ref[:, down_rows - early :] = total(high_ref, high_last_ref, 0, down_rows).T
        write(high_ref, high_last_ref)


def flip(x, axis, bit):
    count = lax.axis_size(axis)
    return lax.ppermute(x, axis, [(i, i ^ bit) for i in range(count)])


def body(tokens, out_grad, routes, gate_probs, w_gate, w_up, w_down):
    tok, width = tokens.shape
    experts = lax.axis_size("expert")
    replicas = lax.axis_size("dp")
    hidden = w_gate.shape[2]
    slots = experts * CAP
    shard = width // replicas
    pieces = replicas // 2
    levels = pieces.bit_length() - 1
    grad_scale = 1.0 / math.sqrt(tok * replicas * experts)
    prob_scale = 1.0 / math.sqrt(width)
    pos = jnp.stack([lax.axis_index("dp"), lax.axis_index("expert")]).astype(jnp.int32)
    chain = []

    def run(kernel, grid, in_specs, out_specs, out_shape, args, after=(), **kw):
        out = call(
            kernel, grid, in_specs, out_specs, out_shape, pos, args, [*chain[-1:], *after], **kw
        )
        chain.append(out[-1])
        return out[:-1]

    def exchange(blocks):
        return [blocks[0]] + [flip(blocks[j], "expert", experts - j) for j in range(1, experts)]

    def block_specs(cols, at):
        return [pl.BlockSpec((CAP, cols), at) for _ in range(experts)]

    def cross(low, high, level):
        return flip(low, "dp", 2 << level), flip(high, "dp", 2 << (levels - 1 - level))

    half = shard // 2
    merged = (shard - FIRST) // 2 + 2 * half

    def add(halves, level, count, places):
        specs, arrays = [], []
        for high, (down, keep, came, *later) in enumerate(halves):

            def spec(size, first, behind, high=high):
                shift = 0 if high else behind
                return pl.BlockSpec(
                    (1, size, hidden),
                    lambda i, pos: (places[high](i) << shift, first, 0),
                )

            specs += [spec(down.shape[1], 0, level - 1)]
            specs += [spec(half, at, level - 1) for at in (0, 0, 1, 1)]
            arrays += [down, keep, came, keep, came]
            for at, array in enumerate(later):
                specs.append(spec(array.shape[1], 0, level - 2 - at))
                arrays.append(array)
        return run(
            add_kernel,
            (count,),
            specs,
            [pl.BlockSpec((1, merged, hidden), lambda i, pos: (i, 0, 0))] * 2,
            [shape_of((count, merged, hidden))] * 2,
            arrays,
        )

    def add_first(low_state, high_state, level):
        count = pieces >> (level + 1)
        places = lambda i: 2 * i + 1, lambda i: count + i
        specs = []
        for high, state in enumerate((low_state, high_state)):
            for at, array in enumerate(state):
                shift = 0 if high else level - 1 - max(at - 1, 0)
                specs.append(
                    pl.BlockSpec(
                        (1, *array.shape[1:]),
                        lambda i, pos, high=high, shift=shift: (places[high](i) << shift, 0, 0),
                    )
                )
        block = (1, FIRST // 2, hidden)
        return run(
            add_all_kernel,
            (count,),
            specs,
            [pl.BlockSpec(block, lambda i, pos: (i, 0, 0))] * 2,
            [shape_of((count, *block[1:]))] * 2,
            low_state + high_state,
        )

    def mark(after, cost):
        run(lambda pos_ref: None, (1,), [], [], [], [], after, cost=cost)

    blocks = [whole((CAP, width)) for _ in range(experts)]
    routes, gate_probs = routes.T, gate_probs.T
    mark([], LONG)
    x_out = run(
        functools.partial(send_tokens_kernel, shard),
        (1,),
        [whole(routes.shape), whole(tokens.shape)],
        [IN_VMEM] * experts,
        [shape_of((CAP, width))] * experts,
        [routes, tokens],
    )
    x_in = exchange(x_out)

    mark([], LONG)

    def send_cot(start, size, after):
        cols = size * replicas
        placed = start == 0
        out = run(
            functools.partial(send_cot_kernel, experts, shard, start),
            (1,),
            [whole(routes.shape), whole(gate_probs.shape), whole(out_grad.shape)],
            [IN_VMEM] * (experts + placed),
            [shape_of((CAP, cols))] * experts + [shape_of((tok, slots))] * placed,
            [routes, gate_probs, out_grad],
            after,
        )
        return exchange(out[:experts]), out[experts:]

    second = shard - FIRST
    dy_first, (place,) = send_cot(0, FIRST, [x_in[1]])
    dy, _ = send_cot(FIRST, second, [])

    def grad_near(rows_t, start, right, others):
        size = (rows_t.shape[0] // replicas - start) // 2 * (right.shape[1] // hidden)
        return run(
            functools.partial(grad_near_kernel, grad_scale, replicas, start),
            (1,),
            [IN_VMEM] * (2 + len(others)),
            [IN_VMEM] * 4,
            [shape_of((pieces // 2, size, hidden))] * 4,
            [rows_t, right, *others],
        )

    def transpose_far(kernel, cols, size, args):
        rows_t, far = run(
            functools.partial(kernel, grad_scale, replicas),
            (1,),
            [IN_VMEM] * len(args),
            [IN_VMEM] * 2,
            [shape_of((cols, slots)), shape_of((pieces * size, hidden))],
            args,
        )
        return rows_t, flip(far, "dp", 1)

    def transpose(rows):
        (out,) = run(
            transpose_kernel,
            (1,),
            [IN_VMEM] * experts,
            [IN_VMEM],
            [shape_of((rows[0].shape[1], slots))],
            rows,
        )
        return out

    act, act_t, for_gate, for_up = run(
        functools.partial(forward_kernel, experts, 3),
        (1,),
        [IN_VMEM] * (experts + 2),
        [IN_VMEM] * 4,
        [shape_of((slots, hidden))] + [shape_of((hidden, slots), t) for t in (BF16, F32, F32)],
        [*x_in, w_gate, w_up],
        scratch=[pltpu.VMEM((slots, width), BF16)],
    )

    first_t, other = transpose_far(
        transpose_far_kernel, replicas * FIRST, FIRST, [act, *dy_first]
    )
    low_send, low_keep, high_send, high_keep = grad_near(first_t, 0, act, [other])
    low, high = cross(low_send, high_send, 0)
    x_t = transpose(x_in)
    low_state, high_state = [low_keep, low], [high_keep, high]
    for level in range(1, levels):
        low, high = cross(*add_first(low_state, high_state, level), level)
        low_state.append(low)
        high_state.append(high)
    (down_first,) = run(
        finish_first_kernel,
        (1,),
        [whole((1, *a.shape[1:])) for a in low_state + high_state],
        [whole((FIRST, hidden))],
        [shape_of((FIRST, hidden), F32)],
        low_state + high_state,
    )

    dy_t, other = transpose_far(transpose_rest_kernel, width, second, [act, first_t, *dy])
    delta, delta_t, prob = run(
        back_hidden_kernel,
        (1,),
        [IN_VMEM] * 5,
        [IN_VMEM] * 3,
        [
            shape_of((slots, 2 * hidden)),
            shape_of((2 * hidden, slots)),
            shape_of((1, slots), F32),
        ],
        [w_down, dy_t, act_t, for_gate, for_up],
    )
    far = run(
        functools.partial(grad_far_kernel, grad_scale, replicas, 0),
        (1,),
        [IN_VMEM] * 2,
        [IN_VMEM] * 3,
        [shape_of((width // 2, 2 * hidden // 3))] * 3,
        [x_t, delta],
    )
    others = [flip(part, "dp", 1) for part in far]
    low_send, low_keep, high_send, high_keep = grad_near(dy_t, FIRST, act, [other])
    down_low, down_high = cross(low_send, high_send, 0)
    down_keep = low_keep, high_keep

    back_out = run(
        row_grad_kernel,
        (1,),
        [IN_VMEM] * 4,
        [IN_VMEM] * experts,
        [shape_of((CAP, width + EXTRA))] * experts,
        [delta_t, prob, w_gate, w_up],
    )
    back_in = exchange(back_out)

    low_send, low_keep, high_send, high_keep = grad_near(x_t, 0, delta, others)
    low, high = cross(low_send, high_send, 0)
    down_low, down_high = run(
        add_pairs_kernel,
        (1,),
        [whole(down_keep[0].shape)] * 4,
        [whole(down_keep[0].shape)] * 2,
        [shape_of(down_keep[0].shape)] * 2,
        [down_keep[0], down_low, down_keep[1], down_high],
    )
    mark([], LONG)
    halves = [[down_low, low_keep, low], [down_high, high_keep, high]]
    for level in range(1, levels):
        count = pieces >> (level + 1)
        places = lambda i: 2 * i + 1, lambda i, count=count: count + i
        low, high = cross(*add(halves, level, count, places), level)
        if level + 1 < levels:
            halves[0].append(low)
            halves[1].append(high)
    mine = add(halves, levels, 1, (lambda i: i, lambda i: i))

    step = width // 2
    x_grad, prob_grad = run(
        functools.partial(combine_kernel, prob_scale),
        (2,),
        [whole((tok, slots)), whole(routes.shape), whole(gate_probs.shape)]
        + block_specs(step, lambda i, pos: (0, i))
        + block_specs(EXTRA, lambda i, pos: (0, width // EXTRA)),
        [pl.BlockSpec((tok, step), lambda i, pos: (0, i)), whole(gate_probs.shape)],
        [shape_of((tok, width)), shape_of(gate_probs.shape)],
        [place, routes, gate_probs, *back_in, *back_in],
        cost=LONG,
    )
    down_grad, gate_grad, up_grad = run(
        finish_kernel,
        (2,),
        [whole(down_first.shape)] + [whole((1, merged, hidden))] * 4,
        [pl.BlockSpec((hidden, half), lambda i, pos: (0, i))]
        + [pl.BlockSpec((half, hidden), lambda i, pos: (i, 0))] * 2,
        [shape_of((hidden, shard), F32)] + [shape_of((shard, hidden), F32)] * 2,
        [down_first, mine[0], low, mine[1], high],
    )
    return (x_grad, prob_grad.T, gate_grad[None], up_grad[None], down_grad[None])


def solution(mesh):
    return jax.shard_map(
        body,
        mesh=mesh,
        in_specs=(
            P(("dp", "expert"), None),
            P(("dp", "expert"), None),
            P(("dp", "expert"), None),
            P(("dp", "expert"), None),
            P("expert", None, None),
            P("expert", None, None),
            P("expert", None, None),
        ),
        out_specs=(
            P(("dp", "expert"), None),
            P(("dp", "expert"), None),
            P("expert", "dp", None),
            P("expert", "dp", None),
            P("expert", None, "dp"),
        ),
        check_vma=False,
    )
```

```python
import functools
import math

import jax
import jax.numpy as jnp
from jax import lax
from jax.experimental import pallas as pl
from jax.experimental.pallas import tpu as pltpu
from jax.sharding import PartitionSpec as P

CAP = 64
FIRST = 128
EXTRA = 128
F32 = jnp.float32
BF16 = jnp.bfloat16
LONG = 6 * 10**10
VMEM_SPARE = 4 * 1024 * 1024


IN_VMEM = pl.BlockSpec(memory_space=pltpu.VMEM)


def whole(shape):
    return pl.BlockSpec(shape, lambda i, pos: (0,) * len(shape))


def call(kernel, grid, in_specs, out_specs, out_shape, pos, args, after, scratch=(), cost=1):
    held = sum(math.prod(ref.shape) * ref.dtype.itemsize for ref in scratch)
    for spec, array in zip([*in_specs, *out_specs], [*args, *out_shape]):
        if spec.block_shape is not None:
            held += 2 * math.prod(spec.block_shape) * array.dtype.itemsize
    first, count, last = 1 + len(args), len(after), len(out_shape)

    def ordered(*refs):
        outs = refs[first + count :]
        kernel(*refs[:first], *outs[:last], *outs[last + 1 :])
        outs[last][...] = jnp.zeros(outs[last].shape, F32)

    return pl.pallas_call(
        ordered,
        grid_spec=pltpu.PrefetchScalarGridSpec(
            num_scalar_prefetch=1,
            grid=grid,
            in_specs=list(in_specs) + [pl.BlockSpec(memory_space=pl.ANY)] * count,
            out_specs=[*out_specs, whole((8, 128))],
            scratch_shapes=list(scratch),
        ),
        out_shape=[*out_shape, shape_of((8, 128), F32)],
        compiler_params=pltpu.CompilerParams(vmem_limit_bytes=held + VMEM_SPARE),
        cost_estimate=pl.CostEstimate(flops=cost, bytes_accessed=1, transcendentals=0),
    )(pos, *args, *after)


def shape_of(shape, dtype=BF16):
    return jax.ShapeDtypeStruct(shape, dtype)


def dot(left, right):
    return jnp.dot(left, right, preferred_element_type=F32)


def shard_rows(relative, pos_ref, stride, start):
    at = (pos_ref[0] ^ relative) * stride + start
    return pl.ds(pl.multiple_of(at, math.gcd(stride, start)), stride - start)


def slot_matrix(routes_ref, my_expert, slots):
    top, tok = routes_ref.shape
    index = lax.broadcasted_iota(jnp.int32, (slots, tok), 0)
    block = index // CAP
    experts = slots // CAP
    turned = jnp.where(block == 1, experts - 2, jnp.where(block == 2, experts - 1, experts - block))
    expert = jnp.where(block == 0, 0, turned) ^ my_expert
    hit = jnp.zeros((slots, tok), jnp.bool_)
    for k in range(top):
        hit = hit | (routes_ref[k : k + 1, :] == expert)
    named = jnp.where(hit, 1.0, 0.0)
    before = lax.broadcasted_iota(jnp.int32, (tok, tok), 0) < lax.broadcasted_iota(
        jnp.int32, (tok, tok), 1
    )
    rank = dot(named.astype(BF16), jnp.where(before, 1.0, 0.0).astype(BF16))
    return jnp.where(rank == (index % CAP).astype(F32), named, 0.0), expert


def send_rows(place, ref, start, shard, outs):
    size = outs[0].shape[1] * shard // ref.shape[1]
    for i in range(ref.shape[1] // shard):
        rows = dot(place, ref[:, i * shard + start : i * shard + start + size]).astype(BF16)
        for j, out_ref in enumerate(outs):
            out_ref[:, i * size : (i + 1) * size] = rows[j * CAP : (j + 1) * CAP]


def send_tokens_kernel(shard, pos_ref, routes_ref, tok_ref, *outs):
    place, _ = slot_matrix(routes_ref, pos_ref[1], len(outs) * CAP)
    send_rows(place.astype(BF16), tok_ref, 0, shard, outs)


def send_cot_kernel(experts, shard, start, pos_ref, routes_ref, probs_ref, cot_ref, *rest):
    outs, place_t_ref = rest[:experts], rest[experts:]
    place, expert = slot_matrix(routes_ref, pos_ref[1], experts * CAP)
    probs = probs_ref[...].astype(F32)
    weight = jnp.zeros_like(place)
    for k in range(routes_ref.shape[0]):
        weight += jnp.where(routes_ref[k : k + 1, :] == expert, probs[k : k + 1, :], 0.0)
    send_rows((place * weight).astype(BF16), cot_ref, start, shard, outs)
    if place_t_ref:
        place_t_ref[0][...] = place.T.astype(BF16)


def joined(refs):
    return jnp.concatenate([ref[...] for ref in refs], axis=0)


def forward_kernel(experts, blocks, pos_ref, *rest):
    xs, (wg_ref, wu_ref), outs, x_ref = (
        rest[:experts],
        rest[experts : experts + 2],
        rest[experts + 2 : -1],
        rest[-1],
    )
    act_ref, act_t_ref, for_gate_ref, for_up_ref = outs
    for j in range(experts):
        x_ref[j * CAP : (j + 1) * CAP, :] = xs[j][...]
    size = wg_ref.shape[2] // blocks
    for i in range(blocks):
        at = slice(i * size, (i + 1) * size)
        gate = dot(x_ref[...], wg_ref[0, :, at]).T
        up = dot(x_ref[...], wu_ref[0, :, at]).T
        sig = jax.nn.sigmoid(gate)
        silu = gate * sig
        act = (silu * up).astype(BF16)
        act_ref[:, at] = act.T
        act_t_ref[at] = act
        for_gate_ref[at] = up * sig * (1.0 + gate * (1.0 - sig))
        for_up_ref[at] = silu


def transpose_kernel(pos_ref, *rest):
    ins, out_ref = rest[:-1], rest[-1]
    size = 512
    for at in range(0, out_ref.shape[0], size):
        rows = [ref[:, at : at + size] for ref in ins]
        out_ref[at : at + size] = jnp.concatenate(rows, axis=0).T


def transpose_far_kernel(scale, replicas, pos_ref, right_ref, *rest):
    ins, (out_ref, far_ref) = rest[:-2], rest[-2:]
    transpose_kernel(pos_ref, *ins, out_ref)
    grad_far_kernel(scale, replicas, 0, pos_ref, out_ref, right_ref, far_ref)


def transpose_rest_kernel(scale, replicas, pos_ref, right_ref, first_ref, *rest):
    ins, (out_ref, far_ref) = rest[:-2], rest[-2:]
    stride = out_ref.shape[0] // replicas
    size = stride - FIRST
    for i in range(replicas):
        at = i * stride
        out_ref[at : at + FIRST] = first_ref[i * FIRST : (i + 1) * FIRST]
        rows = [ref[:, i * size : (i + 1) * size] for ref in ins]
        out_ref[at + FIRST : at + stride] = jnp.concatenate(rows, axis=0).T
    grad_far_kernel(scale, replicas, FIRST, pos_ref, out_ref, right_ref, far_ref)


def grad_far_kernel(scale, replicas, start, pos_ref, rows_ref, right_ref, *outs):
    stride = rows_ref.shape[0] // replicas
    size, cols = stride - start, outs[0].shape[1]
    for i in range(replicas // 2):
        rows = rows_ref[shard_rows(2 * i + 1, pos_ref, stride, start), :]
        part = (dot(rows, right_ref[...]) * scale).astype(BF16)
        for at, out_ref in enumerate(outs):
            out_ref[i * size : (i + 1) * size] = part[:, at * cols : (at + 1) * cols]


def grad_near_kernel(scale, replicas, start, pos_ref, rows_ref, right_ref, *rest):
    others, (low_send, low_keep, high_send, high_keep) = rest[:-4], rest[-4:]
    stride = rows_ref.shape[0] // replicas
    size, cols = stride - start, low_keep.shape[2]
    half, count = size // 2, replicas // 4
    for q in range(replicas // 2):
        rows = rows_ref[shard_rows(2 * q, pos_ref, stride, start), :]
        low_ref = low_send if q % 2 else low_keep
        high_ref, place = (high_send, q - count) if q >= count else (high_keep, q)
        came = [ref[q * size : (q + 1) * size] for ref in others]
        came = jnp.concatenate(came, axis=1).astype(F32)
        total = (dot(rows, right_ref[...]) * scale + came).astype(BF16)
        for at in range(total.shape[1] // cols):
            part = total[:, at * cols : (at + 1) * cols]
            low_ref[q // 2, at * half : (at + 1) * half] = part[:half]
            high_ref[place, at * half : (at + 1) * half] = part[half:]


def back_hidden_kernel(
    pos_ref,
    wd_ref,
    rows_ref,
    act_ref,
    for_gate_ref,
    for_up_ref,
    delta_ref,
    delta_t_ref,
    prob_ref,
):
    back = dot(wd_ref[0], rows_ref[...])
    dh = (back * for_gate_ref[...]).astype(BF16)
    du = (back * for_up_ref[...]).astype(BF16)
    hidden = back.shape[0]
    delta_t_ref[:hidden] = dh
    delta_t_ref[hidden:] = du
    delta_ref[:, :hidden] = dh.T
    delta_ref[:, hidden:] = du.T
    prob_ref[...] = jnp.sum(act_ref[...].astype(F32) * back, axis=0, keepdims=True)


def row_grad_kernel(pos_ref, delta_t_ref, prob_ref, wg_ref, wu_ref, *outs):
    width, hidden = wg_ref.shape[1:]
    size = 512
    for start in range(0, width, size):
        at = slice(start, start + size)
        rows_t = dot(wg_ref[0, at], delta_t_ref[:hidden]) + dot(wu_ref[0, at], delta_t_ref[hidden:])
        rows = rows_t.astype(BF16).T
        for j, out_ref in enumerate(outs):
            out_ref[:, at] = rows[j * CAP : (j + 1) * CAP]
    full = prob_ref[...]
    high = full.astype(BF16).astype(F32)
    lane = lax.broadcasted_iota(jnp.int32, (EXTRA, full.shape[1]), 0)
    both = jnp.where(lane == 0, high, jnp.where(lane == 1, full - high, 0.0)).T.astype(BF16)
    for j, out_ref in enumerate(outs):
        out_ref[:, width:] = both[j * CAP : (j + 1) * CAP]


def total_of(refs):
    down, *rest = [ref[0].astype(F32) for ref in refs]
    first = [down, rest[0] + rest[1], rest[2] + rest[3]]
    return sum(rest[4:], jnp.concatenate(first, axis=0))


def add_kernel(pos_ref, *rest):
    ins, outs = rest[:-2], rest[-2:]
    middle = len(ins) // 2
    for refs, out_ref in zip((ins[:middle], ins[middle:]), outs):
        out_ref[0] = total_of(refs).astype(BF16)


def add_pairs_kernel(pos_ref, a_ref, b_ref, c_ref, d_ref, low_ref, high_ref):
    low_ref[...] = (a_ref[...].astype(F32) + b_ref[...].astype(F32)).astype(BF16)
    high_ref[...] = (c_ref[...].astype(F32) + d_ref[...].astype(F32)).astype(BF16)


def add_all_kernel(pos_ref, *rest):
    ins, outs = rest[:-2], rest[-2:]
    middle = len(ins) // 2
    for refs, out_ref in zip((ins[:middle], ins[middle:]), outs):
        out_ref[...] = sum(ref[...].astype(F32) for ref in refs).astype(BF16)


def finish_first_kernel(pos_ref, *rest):
    ins, out_ref = rest[:-1], rest[-1]
    middle, half = len(ins) // 2, out_ref.shape[0] // 2
    out_ref[:half] = sum(ref[0].astype(F32) for ref in ins[:middle])
    out_ref[half:] = sum(ref[0].astype(F32) for ref in ins[middle:])


def combine_kernel(scale, pos_ref, place_ref, routes_ref, probs_ref, *rest):
    experts = (len(rest) - 2) // 2
    x_ref, prob_ref = rest[2 * experts :]
    rows = joined(rest[:experts])
    x_ref[...] = dot(place_ref[...], rows).astype(BF16)

    @pl.when(pl.program_id(0) == 0)
    def _():
        extra = joined(rest[experts : 2 * experts])
        tok, slots = place_ref.shape
        top = routes_ref.shape[0]
        place, expert = slot_matrix(routes_ref, pos_ref[1], slots)
        value = jnp.sum(extra.astype(F32), axis=1, keepdims=True)
        probs = probs_ref[...].astype(F32)
        line = lax.broadcasted_iota(jnp.int32, probs.shape, 0)
        result = jnp.zeros(probs.shape, F32)
        for k in range(top):
            mine = jnp.where(routes_ref[k : k + 1, :] == expert, place, 0.0)
            found = jnp.sum(mine * value, axis=0, keepdims=True)
            result += jnp.where(line == k, found, 0.0)
        prob_ref[...] = (result * scale / probs).astype(BF16)


def finish_kernel(
    pos_ref, first_ref, low_ref, low_last_ref, high_ref, high_last_ref, down_ref, gate_ref, up_ref
):
    rows = gate_ref.shape[0]
    down_rows = low_ref.shape[1] - 2 * rows
    early = down_ref.shape[1] - FIRST

    def total(ref, last_ref, start, stop):
        return ref[0, start:stop].astype(F32) + last_ref[0, start:stop].astype(F32)

    def write(ref, last_ref):
        gate_ref[...] = total(ref, last_ref, down_rows, down_rows + rows)
        up_ref[...] = total(ref, last_ref, down_rows + rows, down_rows + 2 * rows)

    @pl.when(pl.program_id(0) == 0)
    def _():
        down_ref[:, :FIRST] = first_ref[...].T
        if early:
            down_ref[:, FIRST:] = total(low_ref, low_last_ref, 0, early).T
        write(low_ref, low_last_ref)

    @pl.when(pl.program_id(0) == 1)
    def _():
        down_ref[:, : down_rows - early] = total(low_ref, low_last_ref, early, down_rows).T
        down_ref[:, down_rows - early :] = total(high_ref, high_last_ref, 0, down_rows).T
        write(high_ref, high_last_ref)


def flip(x, axis, bit):
    count = lax.axis_size(axis)
    return lax.ppermute(x, axis, [(i, i ^ bit) for i in range(count)])


def body(tokens, out_grad, routes, gate_probs, w_gate, w_up, w_down):
    tok, width = tokens.shape
    experts = lax.axis_size("expert")
    replicas = lax.axis_size("dp")
    hidden = w_gate.shape[2]
    slots = experts * CAP
    shard = width // replicas
    pieces = replicas // 2
    levels = pieces.bit_length() - 1
    grad_scale = 1.0 / math.sqrt(tok * replicas * experts)
    prob_scale = 1.0 / math.sqrt(width)
    pos = jnp.stack([lax.axis_index("dp"), lax.axis_index("expert")]).astype(jnp.int32)
    chain = []

    def run(kernel, grid, in_specs, out_specs, out_shape, args, after=(), **kw):
        out = call(
            kernel, grid, in_specs, out_specs, out_shape, pos, args, [*chain[-1:], *after], **kw
        )
        chain.append(out[-1])
        return out[:-1]

    def exchange(blocks):
        places = [experts - 2, experts - 1] + [experts - j for j in range(3, experts)]
        moved = [flip(block, "expert", at) for block, at in zip(blocks[1:], places)]
        return [blocks[0]] + moved

    def block_specs(cols, at):
        return [pl.BlockSpec((CAP, cols), at) for _ in range(experts)]

    def cross(low, high, level):
        return flip(low, "dp", 2 << level), flip(high, "dp", 2 << (levels - 1 - level))

    half = shard // 2
    merged = (shard - FIRST) // 2 + 2 * half

    def add(halves, level, count, places):
        specs, arrays = [], []
        for high, (down, keep, came, *later) in enumerate(halves):

            def spec(size, first, behind, high=high):
                shift = 0 if high else behind
                return pl.BlockSpec(
                    (1, size, hidden),
                    lambda i, pos: (places[high](i) << shift, first, 0),
                )

            specs += [spec(down.shape[1], 0, level - 1)]
            specs += [spec(half, at, level - 1) for at in (0, 0, 1, 1)]
            arrays += [down, keep, came, keep, came]
            for at, array in enumerate(later):
                specs.append(spec(array.shape[1], 0, level - 2 - at))
                arrays.append(array)
        return run(
            add_kernel,
            (count,),
            specs,
            [pl.BlockSpec((1, merged, hidden), lambda i, pos: (i, 0, 0))] * 2,
            [shape_of((count, merged, hidden))] * 2,
            arrays,
        )

    def add_first(low_state, high_state, level):
        count = pieces >> (level + 1)
        places = lambda i: 2 * i + 1, lambda i: count + i
        specs = []
        for high, state in enumerate((low_state, high_state)):
            for at, array in enumerate(state):
                shift = 0 if high else level - 1 - max(at - 1, 0)
                specs.append(
                    pl.BlockSpec(
                        (1, *array.shape[1:]),
                        lambda i, pos, high=high, shift=shift: (places[high](i) << shift, 0, 0),
                    )
                )
        block = (1, FIRST // 2, hidden)
        return run(
            add_all_kernel,
            (count,),
            specs,
            [pl.BlockSpec(block, lambda i, pos: (i, 0, 0))] * 2,
            [shape_of((count, *block[1:]))] * 2,
            low_state + high_state,
        )

    def mark(after, cost):
        run(lambda pos_ref: None, (1,), [], [], [], [], after, cost=cost)

    blocks = [whole((CAP, width)) for _ in range(experts)]
    routes, gate_probs = routes.T, gate_probs.T
    mark([], LONG)
    x_out = run(
        functools.partial(send_tokens_kernel, shard),
        (1,),
        [whole(routes.shape), whole(tokens.shape)],
        [IN_VMEM] * experts,
        [shape_of((CAP, width))] * experts,
        [routes, tokens],
    )
    x_in = exchange(x_out)

    mark([], LONG)

    def send_cot(start, size, after):
        cols = size * replicas
        placed = start == 0
        out = run(
            functools.partial(send_cot_kernel, experts, shard, start),
            (1,),
            [whole(routes.shape), whole(gate_probs.shape), whole(out_grad.shape)],
            [IN_VMEM] * (experts + placed),
            [shape_of((CAP, cols))] * experts + [shape_of((tok, slots))] * placed,
            [routes, gate_probs, out_grad],
            after,
        )
        return exchange(out[:experts]), out[experts:]

    second = shard - FIRST
    dy_first, (place,) = send_cot(0, FIRST, [x_in[1]])
    dy, _ = send_cot(FIRST, second, [])

    def grad_near(rows_t, start, right, others):
        size = (rows_t.shape[0] // replicas - start) // 2 * (right.shape[1] // hidden)
        return run(
            functools.partial(grad_near_kernel, grad_scale, replicas, start),
            (1,),
            [IN_VMEM] * (2 + len(others)),
            [IN_VMEM] * 4,
            [shape_of((pieces // 2, size, hidden))] * 4,
            [rows_t, right, *others],
        )

    def transpose_far(kernel, cols, size, args):
        rows_t, far = run(
            functools.partial(kernel, grad_scale, replicas),
            (1,),
            [IN_VMEM] * len(args),
            [IN_VMEM] * 2,
            [shape_of((cols, slots)), shape_of((pieces * size, hidden))],
            args,
        )
        return rows_t, flip(far, "dp", 1)

    def transpose(rows):
        (out,) = run(
            transpose_kernel,
            (1,),
            [IN_VMEM] * experts,
            [IN_VMEM],
            [shape_of((rows[0].shape[1], slots))],
            rows,
        )
        return out

    act, act_t, for_gate, for_up = run(
        functools.partial(forward_kernel, experts, 3),
        (1,),
        [IN_VMEM] * (experts + 2),
        [IN_VMEM] * 4,
        [shape_of((slots, hidden))] + [shape_of((hidden, slots), t) for t in (BF16, F32, F32)],
        [*x_in, w_gate, w_up],
        scratch=[pltpu.VMEM((slots, width), BF16)],
    )

    first_t, other = transpose_far(
        transpose_far_kernel, replicas * FIRST, FIRST, [act, *dy_first]
    )
    low_send, low_keep, high_send, high_keep = grad_near(first_t, 0, act, [other])
    low, high = cross(low_send, high_send, 0)
    x_t = transpose(x_in)
    low_state, high_state = [low_keep, low], [high_keep, high]
    for level in range(1, levels):
        low, high = cross(*add_first(low_state, high_state, level), level)
        low_state.append(low)
        high_state.append(high)
    (down_first,) = run(
        finish_first_kernel,
        (1,),
        [whole((1, *a.shape[1:])) for a in low_state + high_state],
        [whole((FIRST, hidden))],
        [shape_of((FIRST, hidden), F32)],
        low_state + high_state,
    )

    dy_t, other = transpose_far(transpose_rest_kernel, width, second, [act, first_t, *dy])
    delta, delta_t, prob = run(
        back_hidden_kernel,
        (1,),
        [IN_VMEM] * 5,
        [IN_VMEM] * 3,
        [
            shape_of((slots, 2 * hidden)),
            shape_of((2 * hidden, slots)),
            shape_of((1, slots), F32),
        ],
        [w_down, dy_t, act_t, for_gate, for_up],
    )
    far = run(
        functools.partial(grad_far_kernel, grad_scale, replicas, 0),
        (1,),
        [IN_VMEM] * 2,
        [IN_VMEM] * 3,
        [shape_of((width // 2, 2 * hidden // 3))] * 3,
        [x_t, delta],
    )
    others = [flip(part, "dp", 1) for part in far]
    low_send, low_keep, high_send, high_keep = grad_near(dy_t, FIRST, act, [other])
    down_low, down_high = cross(low_send, high_send, 0)
    down_keep = low_keep, high_keep

    back_out = run(
        row_grad_kernel,
        (1,),
        [IN_VMEM] * 4,
        [IN_VMEM] * experts,
        [shape_of((CAP, width + EXTRA))] * experts,
        [delta_t, prob, w_gate, w_up],
    )
    back_in = exchange(back_out)

    low_send, low_keep, high_send, high_keep = grad_near(x_t, 0, delta, others)
    low, high = cross(low_send, high_send, 0)
    down_low, down_high = run(
        add_pairs_kernel,
        (1,),
        [whole(down_keep[0].shape)] * 4,
        [whole(down_keep[0].shape)] * 2,
        [shape_of(down_keep[0].shape)] * 2,
        [down_keep[0], down_low, down_keep[1], down_high],
    )
    mark([], LONG)
    halves = [[down_low, low_keep, low], [down_high, high_keep, high]]
    for level in range(1, levels):
        count = pieces >> (level + 1)
        places = lambda i: 2 * i + 1, lambda i, count=count: count + i
        low, high = cross(*add(halves, level, count, places), level)
        if level + 1 < levels:
            halves[0].append(low)
            halves[1].append(high)
    mine = add(halves, levels, 1, (lambda i: i, lambda i: i))

    step = width // 2
    x_grad, prob_grad = run(
        functools.partial(combine_kernel, prob_scale),
        (2,),
        [whole((tok, slots)), whole(routes.shape), whole(gate_probs.shape)]
        + block_specs(step, lambda i, pos: (0, i))
        + block_specs(EXTRA, lambda i, pos: (0, width // EXTRA)),
        [pl.BlockSpec((tok, step), lambda i, pos: (0, i)), whole(gate_probs.shape)],
        [shape_of((tok, width)), shape_of(gate_probs.shape)],
        [place, routes, gate_probs, *back_in, *back_in],
        cost=LONG,
    )
    down_grad, gate_grad, up_grad = run(
        finish_kernel,
        (2,),
        [whole(down_first.shape)] + [whole((1, merged, hidden))] * 4,
        [pl.BlockSpec((hidden, half), lambda i, pos: (0, i))]
        + [pl.BlockSpec((half, hidden), lambda i, pos: (i, 0))] * 2,
        [shape_of((hidden, shard), F32)] + [shape_of((shard, hidden), F32)] * 2,
        [down_first, mine[0], low, mine[1], high],
    )
    return (x_grad, prob_grad.T, gate_grad[None], up_grad[None], down_grad[None])


def solution(mesh):
    return jax.shard_map(
        body,
        mesh=mesh,
        in_specs=(
            P(("dp", "expert"), None),
            P(("dp", "expert"), None),
            P(("dp", "expert"), None),
            P(("dp", "expert"), None),
            P("expert", None, None),
            P("expert", None, None),
            P("expert", None, None),
        ),
        out_specs=(
            P(("dp", "expert"), None),
            P(("dp", "expert"), None),
            P("expert", "dp", None),
            P("expert", "dp", None),
            P("expert", None, "dp"),
        ),
        check_vma=False,
    )
```
